256 devices in a mesh: rows: 32 (over x, z_lo, core), cols: 8 (over y, z_hi).
Axes of the slice: x: 4, y: 4, z: 8 (z_hi: 2, z_lo: 4; z = z_hi * 4 + z_lo), core: 2. Of those that a mesh axis runs over, the one named last changes fastest.
Arguments:
- density: float32 [8, 1024, 1024], P('cols', 'rows'), may hold values from 0.5 to 2
- velocity: float32 [3, 8, 1024, 1024], P(None, 'cols', 'rows'), may hold values from -2.5 to 2.5
- pressure: float32 [8, 1024, 1024], P('cols', 'rows'), may hold values from 0.5 to 36
- offsets_x: int32 [8, 1024], P('cols', 'rows'), may hold values from -2 to 2
- offsets_y: int32 [8, 1024], P('cols'), may hold values from -2 to 2
Outputs:
- density_out: float32 [8, 1024, 1024], P('cols', 'rows')
- velocity_out: float32 [3, 8, 1024, 1024], P(None, 'cols', 'rows')
- pressure_out: float32 [8, 1024, 1024], P('cols', 'rows')
The draws below stay inside these ranges and needn't reach their ends.
All inputs are finite; a program needn't handle non-finite values.
Results may differ from the reference program's by a relative error of at most 0.0003.
Values sent between devices are 32-bit elements; how exact they have to be, the bound alone decides.
No kernel may reach another device: no remote copies, remote signals or barrier semaphores. Data moves between devices by JAX's collectives and lax.ppermute only.
A program may use at most 64 MiB of HBM per device.

```python
import math
import jax
import jax.numpy as jnp
from jax import lax

SHIFT = 2
NX = 1024
NY = 1024
NZ = 8


def draw_pressure(key, part):
    key = jax.random.fold_in(key, 7)
    level_key = jax.random.fold_in(key, 1)
    field_key = jax.random.fold_in(key, 2)
    heights = jnp.arange(NY, dtype=jnp.float32)[None, :, None] / NY
    top_level = jnp.exp(jax.random.uniform(level_key, (), jnp.float32, math.log(2.5), math.log(5.0)))
    factor = jnp.exp(jax.random.uniform(field_key, (NZ, NY, NX), jnp.float32, math.log(0.5), math.log(2.0)))
    base_level = jnp.exp(jnp.log(top_level) * heights)
    return (base_level * factor).astype(jnp.float32)


def touch_ends(array, key, low, top_value):
    longest = array.shape.index(max(array.shape))
    spots = []
    for shift in (0, 1):
        where = [jax.random.randint(jax.random.fold_in(key, axis), (), 0, length) for axis, length in enumerate(array.shape)]
        where[longest] = (where[longest] + shift) % array.shape[longest]
        spots.append(tuple(where))
    return array.at[spots[0]].set(low).at[spots[1]].set(top_value)


def shard_levels(key, shape, split, low, top_value):
    loudness, own = 1.0, jax.random.fold_in(key, 6)
    for position, parts in split:
        steps = jnp.exp(jax.random.uniform(jax.random.fold_in(own, position), (parts,), jnp.float32, low / len(split), top_value / len(split)))
        loudness = loudness * jnp.repeat(steps, shape[position] // parts).reshape([-1 if axis == position else 1 for axis in range(len(shape))])
    return loudness


def bell_draw(own_key, dims, spread, bound, split=(), kind=jnp.bfloat16):
    values = spread * jax.random.normal(own_key, dims, jnp.float32)
    if split:
        values = values * shard_levels(own_key, dims, split, -0.22, 0.18)
    return jnp.clip(values, -bound, bound).astype(kind)


def setup_inputs(seed: int = 0) -> dict:
    arg_keys = jax.random.split(jax.random.key(seed), 6)
    density = jnp.clip(jnp.exp(math.log(2.0) - 1.3862944 * jax.random.uniform(arg_keys[0], (NZ, NY, NX), jnp.float32) ** shard_levels(arg_keys[0], (NZ, NY, NX), ((0, 8), (1, 32)), -0.2, 0.2)), 0.5, 2.0)
    velocity = bell_draw(arg_keys[1], (3, NZ, NY, NX), 0.5, 2.5, ((1, 8), (2, 32)), jnp.float32)
    pressure = draw_pressure(jax.random.fold_in(arg_keys[5], 71), 0)
    offsets_x = touch_ends(jax.random.randint(arg_keys[3], (NZ, NY), 0 - SHIFT, SHIFT + 1), jax.random.fold_in(arg_keys[3], 1), 0 - SHIFT, SHIFT).astype(jnp.int32)
    offsets_y = touch_ends(jax.random.randint(arg_keys[4], (NZ, NX), 0 - SHIFT, SHIFT + 1), jax.random.fold_in(arg_keys[4], 1), 0 - SHIFT, SHIFT).astype(jnp.int32)
    return {"density": density, "velocity": velocity, "pressure": pressure, "offsets_x": offsets_x, "offsets_y": offsets_y}


courant = 0.4
adiabatic = 5.0 / 3.0

def rolled(values, amount, sweep_axis):
    return jnp.roll(values, amount, axis=sweep_axis)

def profile(values, sweep_axis):
    next_cell = rolled(values, -1, sweep_axis)
    interface = 7.0 / 12.0 * (values + next_cell) - 1.0 / 12.0 * (rolled(values, 1, sweep_axis) + rolled(values, -2, sweep_axis))
    interface = jnp.clip(interface, jnp.minimum(values, next_cell), jnp.maximum(values, next_cell))
    left_gap = rolled(interface, 1, sweep_axis) - values
    right_gap = interface - values
    monotone = left_gap * right_gap < 0.0
    left_edge = values + jnp.where(monotone, jnp.sign(left_gap) * jnp.minimum(jnp.abs(left_gap), 2.0 * jnp.abs(right_gap)), 0.0)
    right_edge = values + jnp.where(monotone, jnp.sign(right_gap) * jnp.minimum(jnp.abs(right_gap), 2.0 * jnp.abs(left_gap)), 0.0)
    return (left_edge, right_edge)

def sweep(density, normal, first_side, second_side, pressure, time_step, sweep_axis):
    sound_speed = jnp.sqrt(adiabatic * pressure / density)
    impedance = density * sound_speed
    vel_left, vel_right = profile(normal, sweep_axis)
    pres_left, pres_right = profile(pressure, sweep_axis)
    imp_next = rolled(impedance, -1, sweep_axis)
    vel_next = rolled(vel_left, -1, sweep_axis)
    pres_next = rolled(pres_left, -1, sweep_axis)
    total_imp = impedance + imp_next
    face_velocity = (impedance * vel_right + imp_next * vel_next + pres_right - pres_next) / total_imp
    face_pressure = (imp_next * pres_right + impedance * pres_next + impedance * imp_next * (vel_right - vel_next)) / total_imp
    displaced = time_step * face_velocity
    widths = 1.0 + displaced - rolled(displaced, 1, sweep_axis)
    work_flux = face_pressure * face_velocity
    lag_density = density / widths
    lag_normal = normal - time_step / density * (face_pressure - rolled(face_pressure, 1, sweep_axis))
    energy = pressure / ((adiabatic - 1.0) * density) + 0.5 * (normal * normal + first_side * first_side + second_side * second_side)
    lag_energy = energy - time_step / density * (work_flux - rolled(work_flux, 1, sweep_axis))
    width_next = rolled(widths, -1, sweep_axis)
    right_part = jnp.maximum(displaced, 0.0) / widths
    left_part = jnp.maximum(-displaced, 0.0) / width_next
    contents = []
    for amount_density in (lag_density, lag_density * lag_normal, lag_density * first_side, lag_density * second_side, lag_density * lag_energy):
        low_edge, high_edge = profile(amount_density, sweep_axis)
        curvature = 6.0 * (amount_density - 0.5 * (low_edge + high_edge))
        slope_gap = high_edge - low_edge
        from_here = high_edge - 0.5 * right_part * (slope_gap - (1.0 - 2.0 / 3.0 * right_part) * curvature)
        from_next = rolled(low_edge, -1, sweep_axis) + 0.5 * left_part * (rolled(slope_gap, -1, sweep_axis) + (1.0 - 2.0 / 3.0 * left_part) * rolled(curvature, -1, sweep_axis))
        face_flux = displaced * jnp.where(displaced > 0.0, from_here, from_next)
        contents.append(amount_density * widths + rolled(face_flux, 1, sweep_axis) - face_flux)
    new_mass, mom_normal, mom_first, mom_second, energy_sum = contents
    kinetic = 0.5 * (mom_normal * mom_normal + mom_first * mom_first + mom_second * mom_second) / new_mass
    new_pressure = (adiabatic - 1.0) * (energy_sum - kinetic)
    return [new_mass, mom_normal / new_mass, mom_first / new_mass, mom_second / new_mass, new_pressure]

def shift_lines(values, offsets, sweep_axis):
    result = jnp.zeros_like(values)
    for amount in range(-SHIFT, SHIFT + 1):
        result = result + jnp.where(offsets == amount, rolled(values, amount, sweep_axis), 0.0)
    return result

def reference(density, velocity, pressure, offsets_x, offsets_y):
    sound_speed = jnp.sqrt(adiabatic * pressure / density)
    signal = jnp.maximum(jnp.abs(velocity[0]), jnp.abs(velocity[1])) + sound_speed
    time_step = courant / jnp.max(signal)

    def plane_step(carried):
        plane_density, plane_velocity, plane_pressure, plane_offx, plane_offy = carried
        fields = sweep(plane_density, plane_velocity[0], plane_velocity[1], plane_velocity[2], plane_pressure, time_step, 1)
        fields = [shift_lines(field_item, plane_offx[:, None], 1) for field_item in fields]
        fields = sweep(fields[0], fields[2], fields[1], fields[3], fields[4], time_step, 0)
        fields = [shift_lines(field_item, plane_offy[None, :], 0) for field_item in fields]
        return (fields[0], jnp.stack([fields[2], fields[1], fields[3]]), fields[4])
    out_density, out_velocity, out_pressure = lax.map(plane_step, (density, jnp.moveaxis(velocity, 1, 0), pressure, offsets_x, offsets_y))
    return (out_density, jnp.moveaxis(out_velocity, 0, 1), out_pressure)
```

```python
import jax
import jax.numpy as jnp
from jax import lax
from jax.experimental import pallas as pl
from jax.experimental.pallas import tpu as pltpu
from jax.sharding import PartitionSpec as P

SHIFT = 2
HALO = 8
LANES = 128
SUB = 8

courant = 0.4
adiabatic = 5.0 / 3.0


def clamp(v, a, b):
    return jnp.minimum(jnp.maximum(v, jnp.minimum(a, b)), jnp.maximum(a, b))


def face_of(am, a0, a1, a2):
    face = 7.0 / 12.0 * (a0 + a1) - 1.0 / 12.0 * (am + a2)
    return clamp(face, a0, a1)


def edges_of(a, face_before, face):
    triple = 3.0 * a
    low = clamp(face_before, a, triple - 2.0 * face)
    high = clamp(face, a, triple - 2.0 * face_before)
    return low, high


def sound_impedance(rho, inv_rho, p):
    return rho * jnp.sqrt(adiabatic * p * inv_rho)


def riemann(z, zn, u_right, u_left, p_right, p_left):
    inv = 1.0 / (z + zn)
    us = (z * u_right + zn * u_left + p_right - p_left) * inv
    ps = (zn * p_right + z * p_left + z * zn * (u_right - u_left)) * inv
    return us, ps


def total_energy(inv_rho, p, un, ta, tb):
    return p * inv_rho * (1.0 / (adiabatic - 1.0)) + 0.5 * (un * un + ta * ta + tb * tb)


def flux_weights(d, f):
    rest = 1.0 - f
    df = d * f
    return d * rest * rest, df * (3.0 - 2.0 * f), df * rest


def primitive(mass, mn, ma, mb, energy):
    inv = 1.0 / mass
    kinetic = 0.5 * (mn * mn + ma * ma + mb * mb) * inv
    return mass, mn * inv, ma * inv, mb * inv, (adiabatic - 1.0) * (energy - kinetic)


def roll_x(v, k):
    return pltpu.roll(v, k % v.shape[1], 1)


def profile_x(a):
    nxt = roll_x(a, -1)
    face = face_of(roll_x(a, 1), a, nxt, roll_x(a, -2))
    low, high = edges_of(a, roll_x(face, 1), face)
    return nxt, low, high


def speed_kernel(den, vel, prs, offx, pay, up, down, row):
    n_rows = den.shape[1]
    peak = None
    for g in range(n_rows // SUB):
        r = pl.ds(g * SUB, SUB)
        c = jnp.sqrt(adiabatic * prs[0, r, :] / den[0, r, :])
        s = jnp.maximum(jnp.abs(vel[0, 0, r, :]), jnp.abs(vel[1, 0, r, :])) + c
        peak = s if peak is None else jnp.maximum(peak, s)
    tile = peak[:, :LANES]
    for k in range(1, peak.shape[1] // LANES):
        tile = jnp.maximum(tile, peak[:, k * LANES : (k + 1) * LANES])
    line = jnp.max(tile, axis=0, keepdims=True)
    line = jnp.maximum(line, pltpu.roll(line, LANES // 2, 1))
    row[...] = jnp.broadcast_to(line, row.shape)
    row[0:1, 0:n_rows] = offx[...].astype(jnp.float32)
    pay[...] = jnp.broadcast_to(row[0:1, :], pay.shape)
    last = pl.ds(n_rows - HALO, HALO)
    first = pl.ds(0, HALO)
    for f, ref in enumerate((den, None, None, None, prs)):
        up[f] = ref[0, last, :] if ref is not None else vel[f - 1, 0, last, :]
        down[f] = ref[0, first, :] if ref is not None else vel[f - 1, 0, first, :]


def face_kernel(den, vel, prs, before, after, state):
    groups = den.shape[1] // SUB + 2
    for g in range(groups):
        if g == 0 or g == groups - 1:
            ref = before if g == 0 else after
            rho, un, ta, tb, p = (ref[f] for f in range(5))
        else:
            r = pl.ds((g - 1) * SUB, SUB)
            rho, p = den[0, r, :], prs[0, r, :]
            un, ta, tb = (vel[f, 0, r, :] for f in range(3))
        inv = 1.0 / rho
        z = sound_impedance(rho, inv, p)
        _, u_low, u_high = profile_x(un)
        _, p_low, p_high = profile_x(p)
        us, ps = riemann(z, roll_x(z, -1), u_high, roll_x(u_low, -1), p_high, roll_x(p_low, -1))
        work = us * ps
        o = pl.ds(g * SUB, SUB)
        state[0, o, :] = rho
        state[1, o, :] = us
        state[2, o, :] = us - roll_x(us, 1)
        state[3, o, :] = un
        state[4, o, :] = (ps - roll_x(ps, 1)) * inv
        state[5, o, :] = ta
        state[6, o, :] = tb
        state[7, o, :] = total_energy(inv, p, un, ta, tb)
        state[8, o, :] = (work - roll_x(work, 1)) * inv


def sweep_kernel(
    n_dev, n_cols, state, got, offy, den_out, vel_out, prs_out,
    pick, pick_s, offy8, swept, rows_out, tiles_out, pick_sem, out_sem,
):
    n_rows, n_x = den_out.shape[1:]
    n_tiles = n_x // LANES
    groups = n_rows // SUB + 2
    me, col = lax.axis_index("rows"), lax.axis_index("cols")
    for k, turn in enumerate((n_dev - 1, 0, 1)):
        pick[k : k + 1, :] = got[pl.ds(lax.rem(me + turn, n_dev) * n_cols + col, 1), :]
    pick_copy = pltpu.make_async_copy(pick, pick_s, pick_sem)
    pick_copy.start()
    for k in range(n_tiles):
        offy8[k : k + 1, :] = offy[:, k * LANES : (k + 1) * LANES]
    lane = lax.broadcasted_iota(jnp.int32, (SUB, LANES), 1)
    top = got[0:SUB, :]
    for k in range(1, got.shape[0] // SUB):
        top = jnp.maximum(top, got[k * SUB : (k + 1) * SUB, :])
    top = jnp.where(lane >= n_rows, top, 0.0)
    dt = courant / jnp.max(jnp.max(top, axis=0, keepdims=True), axis=1, keepdims=True)

    def x_group(g, carry):
        o = pl.ds(pl.multiple_of(g * SUB, SUB), SUB)
        rho, us, dus, un, gp, ta, tb, e, gw = (state[k, o, :] for k in range(9))
        w = 1.0 + dt * dus
        inv_w = 1.0 / w
        up = us > 0.0
        d = dt * us
        k1, k2, k3 = flux_weights(d, jnp.abs(d) * jnp.where(up, inv_w, roll_x(inv_w, -1)))
        lag = rho * inv_w
        contents = []
        for q in (lag, lag * (un - dt * gp), lag * ta, lag * tb, lag * (e - dt * gw)):
            nxt, low, high = profile_x(q)
            near = jnp.where(up, high, roll_x(low, -1))
            far = jnp.where(up, low, roll_x(high, -1))
            flux = k1 * near + k2 * jnp.where(up, q, nxt) - k3 * far
            contents.append(q * w + roll_x(flux, 1) - flux)
        for f, v in enumerate(primitive(*contents)):
            for k in range(n_tiles):
                at = pl.multiple_of((g * n_tiles + k) * SUB, SUB)
                swept[f, pl.ds(at, SUB), :] = v[:, k * LANES : (k + 1) * LANES]
        return carry

    lax.fori_loop(0, groups, x_group, 0)
    pick_copy.wait()

    total = groups * SUB

    def load_row(r):
        if r < HALO:
            s = pick_s[0, n_rows - HALO + r]
        elif r < HALO + n_rows:
            s = pick_s[1, r - HALO]
        else:
            s = pick_s[2, r - HALO - n_rows]
        s = s.astype(jnp.int32)
        turn = lax.rem(s + LANES, LANES)
        step = jnp.where(s > 0, 1, SUB - 1)
        over = lax.shift_right_arithmetic(lane - s, 7) != 0
        fields = []
        for f in range(5):
            at = (r // SUB) * n_tiles * SUB + r % SUB
            v = swept[f, pl.ds(at, SUB, stride=SUB), :]
            v = pltpu.roll(v, turn, 1)
            fields.append(jnp.where(over, pltpu.roll(v, step, 0), v))
        rho, ta, un, tb, p = fields
        return rho, un, ta, tb, p

    oy = offy8[...]
    moved = {k: oy == k for k in range(-SHIFT, SHIFT + 1) if k}
    cells, inv_rho, imp, faces, edges = {}, {}, {}, {}, {}
    stars, lags, weights, q_faces, q_edges, fluxes, done = {}, {}, {}, {}, {}, {}, {}
    copies = []
    for r in range(total):
        cells[r] = load_row(r)
        rho, un, ta, tb, p = cells[r]
        inv_rho[r] = 1.0 / rho
        imp[r] = sound_impedance(rho, inv_rho[r], p)
        i = r - 2
        if i >= 1:
            faces[i] = [face_of(*(cells[i + k][f] for k in (-1, 0, 1, 2))) for f in (1, 4)]
        if i >= 2:
            edges[i] = [edges_of(cells[i][f], faces[i - 1][n], faces[i][n]) for n, f in enumerate((1, 4))]
        i = r - 3
        if i >= 2:
            (_, u_right), (_, p_right) = edges[i]
            (u_left, _), (p_left, _) = edges[i + 1]
            us, ps = riemann(imp[i], imp[i + 1], u_right, u_left, p_right, p_left)
            stars[i] = us, ps, us * ps, dt * us
        if i >= 3:
            rho, un, ta, tb, p = cells[i]
            us, ps, work, d = stars[i]
            _, ps_b, work_b, d_b = stars[i - 1]
            w = 1.0 + d - d_b
            inv_w = 1.0 / w
            rate = dt * inv_rho[i]
            lag = rho * inv_w
            e = total_energy(inv_rho[i], p, un, ta, tb)
            lags[i] = (
                lag, lag * (un - rate * (ps - ps_b)), lag * ta, lag * tb, lag * (e - rate * (work - work_b)),
            )
            weights[i] = w, inv_w
        i = r - 5
        if i >= 4:
            q_faces[i] = [face_of(*(lags[i + k][f] for k in (-1, 0, 1, 2))) for f in range(5)]
        if i >= 5:
            q_edges[i] = [edges_of(lags[i][f], q_faces[i - 1][f], q_faces[i][f]) for f in range(5)]
        i = r - 6
        if i >= 5:
            d = stars[i][3]
            up = d > 0.0
            f_up = jnp.abs(d) * jnp.where(up, weights[i][1], weights[i + 1][1])
            k1, k2, k3 = flux_weights(d, f_up)
            fluxes[i] = []
            for f in range(5):
                low, high = q_edges[i][f]
                low_n, high_n = q_edges[i + 1][f]
                near = jnp.where(up, high, low_n)
                far = jnp.where(up, low, high_n)
                fluxes[i].append(k1 * near + k2 * jnp.where(up, lags[i][f], lags[i + 1][f]) - k3 * far)
        if i >= 6:
            done[i] = primitive(
                *(lags[i][f] * weights[i][0] + fluxes[i - 1][f] - fluxes[i][f] for f in range(5))
            )
        i = r - 8
        if i >= HALO:
            j = i - HALO
            a, b = divmod(j, SUB)
            for f in range(5):
                v = done[i][f]
                for k, mask in moved.items():
                    v = jnp.where(mask, done[i - k][f], v)
                rows_out[f, pl.ds(a * n_tiles * SUB + b, SUB, stride=SUB), :] = v
            if b == SUB - 1:
                for f, ref in enumerate(
                    (den_out.at[0], vel_out.at[1, 0], vel_out.at[0, 0], vel_out.at[2, 0], prs_out.at[0])
                ):
                    here = pl.ds(a * SUB, SUB)
                    for k in range(n_tiles):
                        tiles_out[f, here, pl.ds(k * LANES, LANES)] = rows_out[
                            f, pl.ds((a * n_tiles + k) * SUB, SUB), :
                        ]
                    copies.append(
                        pltpu.make_async_copy(tiles_out.at[f, here, :], ref.at[here, :], out_sem.at[f, a])
                    )
                    copies[-1].start()
    for copy in copies:
        copy.wait()


def body(n_dev, n_cols, density, velocity, pressure, offsets_x, offsets_y):
    n_rows, n_x = density.shape[1:]
    f32 = jnp.float32
    vmem = pl.BlockSpec(memory_space=pltpu.VMEM)
    everyone = n_dev * n_cols
    halo = jax.ShapeDtypeStruct((5, HALO, n_x), f32)
    pay, up, down = pl.pallas_call(
        speed_kernel,
        out_shape=(jax.ShapeDtypeStruct((everyone, LANES), f32), halo, halo),
        in_specs=[vmem] * 4,
        out_specs=[vmem] * 3,
        scratch_shapes=[pltpu.VMEM((SUB, LANES), f32)],
    )(density, velocity, pressure, offsets_x)
    got = lax.all_to_all(pay, ("rows", "cols"), split_axis=0, concat_axis=0, tiled=True)
    before = lax.ppermute(up, "rows", [(i, (i + 1) % n_dev) for i in range(n_dev)])
    after = lax.ppermute(down, "rows", [(i, (i - 1) % n_dev) for i in range(n_dev)])
    total = n_rows + 2 * HALO
    state = pl.pallas_call(
        face_kernel,
        out_shape=jax.ShapeDtypeStruct((9, total, n_x), f32),
        in_specs=[vmem] * 5,
        out_specs=vmem,
        cost_estimate=pl.CostEstimate(flops=total * n_x * 200, bytes_accessed=total * n_x * 64, transcendentals=0),
    )(density, velocity, pressure, before, after)
    plane = jax.ShapeDtypeStruct(density.shape, f32)
    any_space = pl.BlockSpec(memory_space=pl.ANY)
    tall = total * n_x // LANES
    short = n_rows * n_x // LANES
    return pl.pallas_call(
        lambda *refs: sweep_kernel(n_dev, n_cols, *refs),
        out_shape=(plane, jax.ShapeDtypeStruct(velocity.shape, f32), plane),
        in_specs=[vmem] * 3,
        out_specs=[any_space] * 3,
        scratch_shapes=[
            pltpu.VMEM((SUB, LANES), f32),
            pltpu.SMEM((SUB, LANES), f32),
            pltpu.VMEM((n_x // LANES, LANES), jnp.int32),
            pltpu.VMEM((5, tall, LANES), f32),
            pltpu.VMEM((5, short, LANES), f32),
            pltpu.VMEM((5, n_rows, n_x), f32),
            pltpu.SemaphoreType.DMA,
            pltpu.SemaphoreType.DMA((5, n_rows // SUB)),
        ],
    )(state, got, offsets_y)


def solution(mesh):
    n_dev, n_cols = mesh.shape["rows"], mesh.shape["cols"]
    return jax.shard_map(
        lambda *arrays: body(n_dev, n_cols, *arrays),
        mesh=mesh,
        in_specs=(
            P("cols", "rows", None),
            P(None, "cols", "rows", None),
            P("cols", "rows", None),
            P("cols", "rows"),
            P("cols", None),
        ),
        out_specs=(P("cols", "rows", None), P(None, "cols", "rows", None), P("cols", "rows", None)),
        check_vma=False,
    )
```

```python
import jax
import jax.numpy as jnp
from jax import lax
from jax.experimental import pallas as pl
from jax.experimental.pallas import tpu as pltpu
from jax.sharding import PartitionSpec as P

SHIFT = 2
PAIR = 16
REACH = 3
A_LIMIT = 60 * 2**20
OWN_COST = 10**6
HALO_COST = 10**6
HALO = 8
LANES = 128
SUB = 8

courant = 0.4
adiabatic = 5.0 / 3.0


def inverse(v):
    return 1.0 / v


def clamp(v, a, b):
    return jnp.minimum(jnp.maximum(v, jnp.minimum(a, b)), jnp.maximum(a, b))


def face_of(am, a0, a1, a2):
    face = 7.0 / 12.0 * (a0 + a1) - 1.0 / 12.0 * (am + a2)
    return clamp(face, a0, a1)


def edges_of(a, face_before, face):
    triple = 3.0 * a
    low = clamp(face_before, a, triple - 2.0 * face)
    high = clamp(face, a, triple - 2.0 * face_before)
    return low, high


def sound_impedance(rho, inv_rho, p):
    return rho * jnp.sqrt(adiabatic * p * inv_rho)


def riemann(z, zn, u_right, u_left, p_right, p_left):
    inv = inverse(z + zn)
    us = (z * u_right + zn * u_left + p_right - p_left) * inv
    ps = (zn * p_right + z * p_left + z * zn * (u_right - u_left)) * inv
    return us, ps


def total_energy(inv_rho, p, un, ta, tb):
    return p * inv_rho * (1.0 / (adiabatic - 1.0)) + 0.5 * (un * un + ta * ta + tb * tb)


def flux_weights(d, f):
    rest = 1.0 - f
    df = d * f
    return d * rest * rest, df * (3.0 - 2.0 * f), df * rest


def primitive(mass, mn, ma, mb, energy):
    inv = inverse(mass)
    kinetic = 0.5 * (mn * mn + ma * ma + mb * mb) * inv
    return mass, mn * inv, ma * inv, mb * inv, (adiabatic - 1.0) * (energy - kinetic)


def split(v):
    return [v[:, k : k + LANES] for k in range(0, v.shape[1], LANES)]


def to_columns(halves, room):
    rows = [half[:, k : k + LANES] for k in range(0, halves[0].shape[1], LANES) for half in halves]
    room[...] = jnp.transpose(jnp.concatenate(rows, axis=0))
    return [room[pl.ds(j, SUB, stride=LANES // SUB), :] for j in range(LANES // SUB)]


def wrapped(tile, way):
    sub = lax.broadcasted_iota(jnp.int32, tile.shape, 0)
    turned = pltpu.roll(tile, way % SUB, 0)
    edge = 0 if way > 0 else SUB - 1
    return jnp.where(sub == edge, pltpu.roll(turned, way * PAIR % LANES, 1), turned)


def roll_x(v, k):
    parts = split(v)
    n = len(parts)
    moved = []
    for j in range(n):
        turns, source = divmod(j - k, n)
        moved.append(parts[source] if turns == 0 else wrapped(parts[source], -turns))
    return jnp.concatenate(moved, axis=1)


def profile_x(a):
    nxt = roll_x(a, -1)
    face = face_of(roll_x(a, 1), a, nxt, roll_x(a, -2))
    low, high = edges_of(a, roll_x(face, 1), face)
    return nxt, low, high


def lines_of(offx, first):
    shape = (SUB, LANES)
    lane = lax.broadcasted_iota(jnp.int32, shape, 1)
    row = lax.broadcasted_iota(jnp.int32, shape, 0)
    found = jnp.where(lane == row + first, jnp.broadcast_to(offx, shape), 0.0)
    return jnp.broadcast_to(jnp.sum(found, axis=1, keepdims=True), shape)


def speed_kernel(den, vel, prs, offx_hbm, pay, up, down, block, offx, line, sems, pack_sems):
    n_rows, n_x = den.shape[1:]
    off_load = pltpu.make_async_copy(offx_hbm, offx, sems.at[5])
    sources = (den.at[0], vel.at[0, 0], vel.at[1, 0], vel.at[2, 0], prs.at[0])
    loads = [pltpu.make_async_copy(sources[f], block.at[:, pl.ds(f * n_x, n_x)], sems.at[f]) for f in range(5)]
    for load in (*loads, off_load):
        load.start()
    line[...] = jnp.zeros_like(line)
    off_load.wait()
    line[:, 0:n_rows] = offx[...].astype(jnp.float32)
    for first in (0, n_rows - HALO):
        block[first : first + HALO, 5 * n_x :] = lines_of(line[...], first)
    for load in loads:
        load.wait()
    packs = [
        pltpu.make_async_copy(block.at[pl.ds(first, HALO), :], out, pack_sems.at[k])
        for k, (out, first) in enumerate(((up, n_rows - HALO), (down, 0)))
    ]
    for pack in packs:
        pack.start()
    peak = None
    for g in range(n_rows // SUB):
        rho, un, ta, p = (block[g * SUB : (g + 1) * SUB, f * n_x : (f + 1) * n_x] for f in (0, 1, 2, 4))
        s = jnp.maximum(jnp.abs(un), jnp.abs(ta)) + jnp.sqrt(adiabatic * p / rho)
        peak = s if peak is None else jnp.maximum(peak, s)
    tiles = split(peak)
    while len(tiles) > 1:
        tiles = [jnp.maximum(x, y) for x, y in zip(tiles[::2], tiles[1::2])]
    pay[...] = jnp.broadcast_to(jnp.max(tiles[0], axis=0, keepdims=True), pay.shape)
    for pack in packs:
        pack.wait()


def prepare(halves, state, row, by, rooms):
    rho, un, ta, tb, p = (
        jnp.concatenate(to_columns([h[f] for h in halves], rooms.at[f]), axis=1) for f in range(5)
    )
    lines = jnp.concatenate([h[5] for h in halves] * (LANES // PAIR), axis=0)
    by[pl.ds(row, SUB), :] = jnp.transpose(lines)[0:SUB, :]
    inv = inverse(rho)
    z = sound_impedance(rho, inv, p)
    _, u_low, u_high = profile_x(un)
    _, p_low, p_high = profile_x(p)
    us, ps = riemann(z, roll_x(z, -1), u_high, roll_x(u_low, -1), p_high, roll_x(p_low, -1))
    work = us * ps
    o = pl.ds(row, SUB)
    values = (
        rho, us, us - roll_x(us, 1), un, (ps - roll_x(ps, 1)) * inv, ta, tb,
        total_energy(inv, p, un, ta, tb), (work - roll_x(work, 1)) * inv,
    )
    for n, v in enumerate(values):
        tiles = split(v)
        ends = [wrapped(t, 1) for t in tiles[-REACH:]], [wrapped(t, -1) for t in tiles[:REACH]]
        for t, tile in enumerate(ends[0] + tiles + ends[1]):
            state[n, o, t * LANES : (t + 1) * LANES] = tile


def own_kernel(den, vel, prs, offx, offy, state, rows_by, lines_by, line, rooms):
    n_rows, n_x = den.shape[1:]
    for k in range(n_x // LANES):
        lines_by[k : k + 1, :] = offy[:, k * LANES : (k + 1) * LANES].astype(jnp.float32)
    line[...] = jnp.zeros_like(line)
    line[:, 0:n_rows] = offx[...].astype(jnp.float32)
    for g in range(n_rows // PAIR):
        halves = []
        for first in range(g * PAIR, (g + 1) * PAIR, SUB):
            r = pl.ds(first, SUB)
            halves.append(
                [den[0, r, :], vel[0, 0, r, :], vel[1, 0, r, :], vel[2, 0, r, :], prs[0, r, :], lines_of(line[...], first)]
            )
        prepare(halves, state, g * SUB, rows_by, rooms.at[g])


def halo_kernel(before, after, state, rows_by, rooms):
    n_x = (before.shape[1] - LANES) // 5
    halves = [[ref[:, f * n_x : (f + 1) * n_x] for f in range(5)] + [ref[:, 5 * n_x :]] for ref in (before, after)]
    prepare(halves, state, 0, rows_by, rooms)


def sweep_kernel(
    state, halo_state, got, rows_by, halo_by, lines_by, den_out, vel_out, prs_out,
    columns, swept, rows_out, tiles_out, out_sem,
):
    n_rows, n_x = den_out.shape[1:]
    n_tiles = n_x // LANES
    groups = n_rows // SUB + 2
    n_steps = LANES // SUB
    top = [got[k * SUB : (k + 1) * SUB, :] for k in range(got.shape[0] // SUB)]
    while len(top) > 1:
        top = [jnp.maximum(x, y) for x, y in zip(top[::2], top[1::2])]
    dt = courant / jnp.max(jnp.max(top[0], axis=0, keepdims=True), axis=1, keepdims=True)

    def x_group(state, row, offsets, n, late):
        o = pl.ds(row, SUB)

        def tile_of(n, t):
            return state[n, o, (t + REACH) * LANES : (t + REACH + 1) * LANES]

        width, inv_w, amount, face, edges, flux, result = {}, {}, {}, {}, {}, {}, {}
        shifted = {k: offsets == k for k in range(-SHIFT, SHIFT + 1) if k}

        def put(j):
            for f in range(5):
                v = result[j][f]
                for k, mask in shifted.items():
                    v = jnp.where(mask, result[j - k][f], v)
                columns[n, f, pl.ds(j, SUB, stride=n_steps), :] = v

        for t in range(-REACH, n_steps + REACH):
            width[t] = 1.0 + dt * tile_of(2, t)
            inv_w[t] = inverse(width[t])
            lag = tile_of(0, t) * inv_w[t]
            amount[t] = (
                lag, lag * (tile_of(3, t) - dt * tile_of(4, t)), lag * tile_of(5, t), lag * tile_of(6, t),
                lag * (tile_of(7, t) - dt * tile_of(8, t)),
            )
            if late:
                late.pop(0)()
            i = t - 2
            if i >= -2:
                face[i] = [face_of(*(amount[i + k][f] for k in (-1, 0, 1, 2))) for f in range(5)]
            if i >= -1:
                edges[i] = [edges_of(amount[i][f], face[i - 1][f], face[i][f]) for f in range(5)]
            i = t - 3
            if i >= -1:
                us = tile_of(1, i)
                up = us > 0.0
                d = dt * us
                k1, k2, k3 = flux_weights(d, jnp.abs(d) * jnp.where(up, inv_w[i], inv_w[i + 1]))
                flux[i] = []
                for f in range(5):
                    (low, high), (low_n, high_n) = edges[i][f], edges[i + 1][f]
                    near = jnp.where(up, high, low_n)
                    far = jnp.where(up, low, high_n)
                    mean = jnp.where(up, amount[i][f], amount[i + 1][f])
                    flux[i].append(k1 * near + k2 * mean - k3 * far)
            if i >= 0:
                kept = [tile_of(0, i)] + [amount[i][f] * width[i] for f in range(1, 5)]
                result[i] = primitive(*(kept[f] + flux[i - 1][f] - flux[i][f] for f in range(5)))
                if i < SHIFT:
                    result[n_steps + i] = [wrapped(v, -1) for v in result[i]]
                if i >= n_steps - SHIFT:
                    result[i - n_steps] = [wrapped(v, 1) for v in result[i]]
                if i >= 2 * SHIFT:
                    put(i - SHIFT)
        for j in (n_steps - 2, n_steps - 1, 0, 1):
            late.append(lambda j=j: put(j))

    def turn(n, f, first, second):
        natural = jnp.transpose(columns[n, f])
        for k in range(n_tiles):
            for h, group in enumerate((first, second)):
                at = (k * 2 + h) * SUB
                swept[f, pl.ds((group * n_tiles + k) * SUB, SUB), :] = natural[at : at + SUB, :]

    n_own = n_rows // PAIR
    late, turns = [], []
    x_group(halo_state, 0, halo_by[...], 0, late)
    for g in range(n_own):
        x_group(state, g * SUB, rows_by[g * SUB : (g + 1) * SUB, :], g + 1, late)
        if g == 0:
            turns = [(0, f, 0, groups - 1) for f in range(5)]
        else:
            turns = [(g, f, 2 * g - 1, 2 * g) for f in range(5)]
        for args in turns:
            turn(*args)
    for put_late in late:
        put_late()
    turns = [(n_own, f, 2 * n_own - 1, 2 * n_own) for f in range(5)]

    total = groups * SUB

    def load_row(r):
        at = (r // SUB) * n_tiles * SUB + r % SUB
        rho, ta, un, tb, p = (swept[f, pl.ds(at, SUB, stride=SUB), :] for f in range(5))
        return rho, un, ta, tb, p

    oy = lines_by[...]
    moved = {k: oy == k for k in range(-SHIFT, SHIFT + 1) if k}
    cells, inv_rho, imp, faces, edges = {}, {}, {}, {}, {}
    stars, lags, weights, q_faces, q_edges, fluxes, done = {}, {}, {}, {}, {}, {}, {}
    copies, waiting = [], []
    targets = (den_out.at[0], vel_out.at[1, 0], vel_out.at[0, 0], vel_out.at[2, 0], prs_out.at[0])

    def turn_back(a, f):
        here = pl.ds(a * SUB, SUB)
        tiles = [rows_out[f, pl.ds((a * n_tiles + j) * SUB, SUB), :] for j in range(n_tiles)]
        for k, tile in enumerate(tiles):
            tiles_out[f, here, pl.ds(k * LANES, LANES)] = tile

    def send(a):
        here = pl.ds(a * SUB, SUB)
        for f in range(5):
            copies.append(
                pltpu.make_async_copy(tiles_out.at[f, here, :], targets[f].at[here, :], out_sem.at[f, a])
            )
            copies[-1].start()

    for r in range(total):
        if turns:
            turn(*turns.pop(0))
        cells[r] = load_row(r)
        rho, un, ta, tb, p = cells[r]
        inv_rho[r] = inverse(rho)
        imp[r] = sound_impedance(rho, inv_rho[r], p)
        i = r - 2
        if i >= 1:
            faces[i] = [face_of(*(cells[i + k][f] for k in (-1, 0, 1, 2))) for f in (1, 4)]
        if i >= 2:
            edges[i] = [edges_of(cells[i][f], faces[i - 1][n], faces[i][n]) for n, f in enumerate((1, 4))]
        i = r - 3
        if i >= 2:
            (_, u_right), (_, p_right) = edges[i]
            (u_left, _), (p_left, _) = edges[i + 1]
            us, ps = riemann(imp[i], imp[i + 1], u_right, u_left, p_right, p_left)
            stars[i] = us, ps, us * ps, dt * us
        if i >= 3:
            rho, un, ta, tb, p = cells[i]
            us, ps, work, d = stars[i]
            _, ps_b, work_b, d_b = stars[i - 1]
            w = 1.0 + d - d_b
            inv_w = inverse(w)
            rate = dt * inv_rho[i]
            lag = rho * inv_w
            e = total_energy(inv_rho[i], p, un, ta, tb)
            lags[i] = (
                lag, lag * (un - rate * (ps - ps_b)), lag * ta, lag * tb, lag * (e - rate * (work - work_b)),
            )
            weights[i] = w, inv_w
        i = r - 5
        if i >= 4:
            q_faces[i] = [face_of(*(lags[i + k][f] for k in (-1, 0, 1, 2))) for f in range(5)]
        if i >= 5:
            q_edges[i] = [edges_of(lags[i][f], q_faces[i - 1][f], q_faces[i][f]) for f in range(5)]
        i = r - 6
        if i >= 5:
            d = stars[i][3]
            up = d > 0.0
            f_up = jnp.abs(d) * jnp.where(up, weights[i][1], weights[i + 1][1])
            k1, k2, k3 = flux_weights(d, f_up)
            fluxes[i] = []
            for f in range(5):
                low, high = q_edges[i][f]
                low_n, high_n = q_edges[i + 1][f]
                near = jnp.where(up, high, low_n)
                far = jnp.where(up, low, high_n)
                fluxes[i].append(k1 * near + k2 * jnp.where(up, lags[i][f], lags[i + 1][f]) - k3 * far)
        if i >= 6:
            done[i] = primitive(
                *(lags[i][f] * weights[i][0] + fluxes[i - 1][f] - fluxes[i][f] for f in range(5))
            )
        i = r - 8
        if i >= HALO:
            j = i - HALO
            a, b = divmod(j, SUB)
            for f in range(5):
                v = done[i][f]
                for k, mask in moved.items():
                    v = jnp.where(mask, done[i - k][f], v)
                rows_out[f, pl.ds(a * n_tiles * SUB + b, SUB, stride=SUB), :] = v
            if b == SUB - 1:
                if a:
                    send(a - 1)
                waiting += [(a, f) for f in range(5)]
        if waiting:
            turn_back(*waiting.pop(0))
    for a, f in waiting:
        turn_back(a, f)
    send(n_rows // SUB - 1)
    for copy in copies:
        copy.wait()


def body(n_dev, n_cols, density, velocity, pressure, offsets_x, offsets_y):
    n_rows, n_x = density.shape[1:]
    f32 = jnp.float32
    vmem = pl.BlockSpec(memory_space=pltpu.VMEM)
    everyone = n_dev * n_cols
    small = pltpu.CompilerParams(vmem_limit_bytes=16 * 2**20)
    hbm = pl.BlockSpec(memory_space=pltpu.HBM)
    wide = 5 * n_x + LANES
    halo = jax.ShapeDtypeStruct((HALO, wide), f32)
    pay, up, down = pl.pallas_call(
        speed_kernel,
        out_shape=(jax.ShapeDtypeStruct((everyone, LANES), f32), halo, halo),
        in_specs=[hbm] * 4,
        out_specs=[vmem] + [hbm] * 2,
        scratch_shapes=[
            pltpu.VMEM((n_rows, wide), f32),
            pltpu.VMEM(offsets_x.shape, jnp.int32),
            pltpu.VMEM((1, LANES), f32),
            pltpu.SemaphoreType.DMA((6,)),
            pltpu.SemaphoreType.DMA((2,)),
        ],
        compiler_params=pltpu.CompilerParams(vmem_limit_bytes=A_LIMIT),
    )(density, velocity, pressure, offsets_x)
    got = lax.all_to_all(pay, ("rows", "cols"), split_axis=0, concat_axis=0, tiled=True)
    before = lax.ppermute(up, "rows", [(i, (i + 1) % n_dev) for i in range(n_dev)])
    after = lax.ppermute(down, "rows", [(i, (i - 1) % n_dev) for i in range(n_dev)])
    long = (LANES // SUB + 2 * REACH) * LANES
    rooms = pltpu.VMEM((5, LANES, LANES), f32)
    n_own = n_rows // PAIR
    state, rows_by, lines_by = pl.pallas_call(
        own_kernel,
        out_shape=(
            jax.ShapeDtypeStruct((9, n_own * SUB, long), f32),
            jax.ShapeDtypeStruct((n_own * SUB, LANES), f32),
            jax.ShapeDtypeStruct((SUB, LANES), f32),
        ),
        in_specs=[vmem] * 5,
        out_specs=[vmem] * 3,
        scratch_shapes=[pltpu.VMEM((1, LANES), f32), pltpu.VMEM((n_own, 5, LANES, LANES), f32)],
        compiler_params=small,
        cost_estimate=pl.CostEstimate(flops=OWN_COST, bytes_accessed=10**6, transcendentals=0),
    )(density, velocity, pressure, offsets_x, offsets_y)
    halo_state, halo_by = pl.pallas_call(
        halo_kernel,
        out_shape=(
            jax.ShapeDtypeStruct((9, SUB, long), f32), jax.ShapeDtypeStruct((SUB, LANES), f32),
        ),
        in_specs=[vmem] * 2,
        out_specs=[vmem] * 2,
        scratch_shapes=[rooms],
        compiler_params=small,
        cost_estimate=pl.CostEstimate(flops=HALO_COST, bytes_accessed=10**6, transcendentals=0),
    )(before, after)
    plane = jax.ShapeDtypeStruct(density.shape, f32)
    tall = (n_rows + 2 * HALO) * n_x // LANES
    short = n_rows * n_x // LANES
    return pl.pallas_call(
        sweep_kernel,
        out_shape=(plane, jax.ShapeDtypeStruct(velocity.shape, f32), plane),
        in_specs=[vmem] * 6,
        out_specs=[hbm] * 3,
        scratch_shapes=[
            pltpu.VMEM((n_own + 1, 5, LANES, LANES), f32),
            pltpu.VMEM((5, tall, LANES), f32),
            pltpu.VMEM((5, short, LANES), f32),
            pltpu.VMEM((5, n_rows, n_x), f32),
            pltpu.SemaphoreType.DMA((5, n_rows // SUB)),
        ],
        compiler_params=small,
    )(state, halo_state, got, rows_by, halo_by, lines_by)


def solution(mesh):
    n_dev, n_cols = mesh.shape["rows"], mesh.shape["cols"]
    return jax.shard_map(
        lambda *arrays: body(n_dev, n_cols, *arrays),
        mesh=mesh,
        in_specs=(
            P("cols", "rows", None),
            P(None, "cols", "rows", None),
            P("cols", "rows", None),
            P("cols", "rows"),
            P("cols", None),
        ),
        out_specs=(P("cols", "rows", None), P(None, "cols", "rows", None), P("cols", "rows", None)),
        check_vma=False,
    )
```

```python
import jax
import jax.numpy as jnp
from jax import lax
from jax.experimental import pallas as pl
from jax.experimental.pallas import tpu as pltpu
from jax.sharding import PartitionSpec as P

SHIFT = 2
PAIR = 16
REACH = 3
A_LIMIT = 60 * 2**20
OWN_COST = 10**6
HALO_COST = 10**6
LEAD = 16
HALO = 8
LANES = 128
SUB = 8

courant = 0.4
adiabatic = 5.0 / 3.0


def inverse(v):
    return 1.0 / v


def clamp(v, a, b):
    return jnp.minimum(jnp.maximum(v, jnp.minimum(a, b)), jnp.maximum(a, b))


def face_of(am, a0, a1, a2):
    face = 7.0 / 12.0 * (a0 + a1) - 1.0 / 12.0 * (am + a2)
    return clamp(face, a0, a1)


def edges_of(a, face_before, face):
    triple = 3.0 * a
    low = clamp(face_before, a, triple - 2.0 * face)
    high = clamp(face, a, triple - 2.0 * face_before)
    return low, high


def sound_impedance(rho, inv_rho, p):
    return rho * jnp.sqrt(adiabatic * p * inv_rho)


def riemann(z, zn, u_right, u_left, p_right, p_left):
    inv = inverse(z + zn)
    us = (z * u_right + zn * u_left + p_right - p_left) * inv
    ps = (zn * p_right + z * p_left + z * zn * (u_right - u_left)) * inv
    return us, ps


def total_energy(inv_rho, p, un, ta, tb):
    return p * inv_rho * (1.0 / (adiabatic - 1.0)) + 0.5 * (un * un + ta * ta + tb * tb)


def flux_weights(d, f):
    rest = 1.0 - f
    df = d * f
    return d * rest * rest, df * (3.0 - 2.0 * f), df * rest


def primitive(mass, mn, ma, mb, energy):
    inv = inverse(mass)
    kinetic = 0.5 * (mn * mn + ma * ma + mb * mb) * inv
    return mass, mn * inv, ma * inv, mb * inv, (adiabatic - 1.0) * (energy - kinetic)


def split(v):
    return [v[:, k : k + LANES] for k in range(0, v.shape[1], LANES)]


def to_columns(halves, room):
    rows = [half[:, k : k + LANES] for k in range(0, halves[0].shape[1], LANES) for half in halves]
    room[...] = jnp.transpose(jnp.concatenate(rows, axis=0))
    return [room[pl.ds(j, SUB, stride=LANES // SUB), :] for j in range(LANES // SUB)]


def wrapped(tile, way):
    sub = lax.broadcasted_iota(jnp.int32, tile.shape, 0)
    turned = pltpu.roll(tile, way % SUB, 0)
    edge = 0 if way > 0 else SUB - 1
    return jnp.where(sub == edge, pltpu.roll(turned, way * PAIR % LANES, 1), turned)


def roll_x(v, k):
    parts = split(v)
    n = len(parts)
    moved = []
    for j in range(n):
        turns, source = divmod(j - k, n)
        moved.append(parts[source] if turns == 0 else wrapped(parts[source], -turns))
    return jnp.concatenate(moved, axis=1)


def profile_x(a):
    nxt = roll_x(a, -1)
    face = face_of(roll_x(a, 1), a, nxt, roll_x(a, -2))
    low, high = edges_of(a, roll_x(face, 1), face)
    return nxt, low, high


def lines_of(offx, first):
    shape = (SUB, LANES)
    lane = lax.broadcasted_iota(jnp.int32, shape, 1)
    row = lax.broadcasted_iota(jnp.int32, shape, 0)
    found = jnp.where(lane == row + first, jnp.broadcast_to(offx, shape), 0.0)
    return jnp.broadcast_to(jnp.sum(found, axis=1, keepdims=True), shape)


def speed_kernel(den, vel, prs, offx_hbm, pay_hbm, up, down, pay, block, offx, line, sems, pack_sems):
    n_rows, n_x = den.shape[1:]
    off_load = pltpu.make_async_copy(offx_hbm, offx, sems.at[5])
    sources = (den.at[0], vel.at[0, 0], vel.at[1, 0], vel.at[2, 0], prs.at[0])
    loads = [pltpu.make_async_copy(sources[f], block.at[:, pl.ds(f * n_x, n_x)], sems.at[f]) for f in range(5)]
    for load in (*loads, off_load):
        load.start()
    line[...] = jnp.zeros_like(line)
    off_load.wait()
    line[:, 0:n_rows] = offx[...].astype(jnp.float32)
    for first in (0, n_rows - HALO):
        block[first : first + HALO, 5 * n_x :] = lines_of(line[...], first)
    for load in loads:
        load.wait()
    packs = [
        pltpu.make_async_copy(block.at[pl.ds(first, HALO), :], out, pack_sems.at[k])
        for k, (out, first) in enumerate(((up, n_rows - HALO), (down, 0)))
    ]
    for pack in packs:
        pack.start()
    peak = None
    for g in range(n_rows // SUB):
        rho, un, ta, p = (block[g * SUB : (g + 1) * SUB, f * n_x : (f + 1) * n_x] for f in (0, 1, 2, 4))
        s = jnp.maximum(jnp.abs(un), jnp.abs(ta)) + jnp.sqrt(adiabatic * p / rho)
        peak = s if peak is None else jnp.maximum(peak, s)
    tiles = split(peak)
    while len(tiles) > 1:
        tiles = [jnp.maximum(x, y) for x, y in zip(tiles[::2], tiles[1::2])]
    pay[...] = jnp.broadcast_to(jnp.max(tiles[0], axis=0, keepdims=True), pay.shape)
    packs.append(pltpu.make_async_copy(pay, pay_hbm, pack_sems.at[2]))
    packs[-1].start()
    for pack in packs:
        pack.wait()


def prepare(halves, state, row, by, rooms):
    rho, un, ta, tb, p = (
        jnp.concatenate(to_columns([h[f] for h in halves], rooms.at[f]), axis=1) for f in range(5)
    )
    lines = jnp.concatenate([h[5] for h in halves] * (LANES // PAIR), axis=0)
    by[pl.ds(row, SUB), :] = jnp.transpose(lines)[0:SUB, :]
    inv = inverse(rho)
    z = sound_impedance(rho, inv, p)
    _, u_low, u_high = profile_x(un)
    _, p_low, p_high = profile_x(p)
    us, ps = riemann(z, roll_x(z, -1), u_high, roll_x(u_low, -1), p_high, roll_x(p_low, -1))
    work = us * ps
    o = pl.ds(row, SUB)
    values = (
        rho, us, us - roll_x(us, 1), un, (ps - roll_x(ps, 1)) * inv, ta, tb,
        total_energy(inv, p, un, ta, tb), (work - roll_x(work, 1)) * inv,
    )
    for n, v in enumerate(values):
        tiles = split(v)
        ends = [wrapped(t, 1) for t in tiles[-REACH:]], [wrapped(t, -1) for t in tiles[:REACH]]
        for t, tile in enumerate(ends[0] + tiles + ends[1]):
            state[n, o, t * LANES : (t + 1) * LANES] = tile


def own_kernel(den, vel, prs, offx, offy, state, rows_by, lines_by, line, rooms):
    n_rows, n_x = den.shape[1:]
    for k in range(n_x // LANES):
        lines_by[k : k + 1, :] = offy[:, k * LANES : (k + 1) * LANES].astype(jnp.float32)
    line[...] = jnp.zeros_like(line)
    line[:, 0:n_rows] = offx[...].astype(jnp.float32)
    for g in range(n_rows // PAIR):
        halves = []
        for first in range(g * PAIR, (g + 1) * PAIR, SUB):
            r = pl.ds(first, SUB)
            halves.append(
                [den[0, r, :], vel[0, 0, r, :], vel[1, 0, r, :], vel[2, 0, r, :], prs[0, r, :], lines_of(line[...], first)]
            )
        prepare(halves, state, g * SUB, rows_by, rooms.at[g])


def halo_kernel(before, after, state, rows_by, rooms):
    n_x = (before.shape[1] - LANES) // 5
    halves = [[ref[:, f * n_x : (f + 1) * n_x] for f in range(5)] + [ref[:, 5 * n_x :]] for ref in (before, after)]
    prepare(halves, state, 0, rows_by, rooms)


def sweep_kernel(
    state, halo_state, got, rows_by, halo_by, lines_by, den_out, vel_out, prs_out,
    columns, swept, rows_out, tiles_out, out_sem,
):
    n_rows, n_x = den_out.shape[1:]
    n_tiles = n_x // LANES
    groups = n_rows // SUB + 2
    n_steps = LANES // SUB
    top = [got[k * SUB : (k + 1) * SUB, :] for k in range(got.shape[0] // SUB)]
    while len(top) > 1:
        top = [jnp.maximum(x, y) for x, y in zip(top[::2], top[1::2])]
    dt = courant / jnp.max(jnp.max(top[0], axis=0, keepdims=True), axis=1, keepdims=True)

    def x_group(state, row, offsets, block, late):
        o = pl.ds(row, SUB)

        def tile_of(n, t):
            return state[n, o, (t + REACH) * LANES : (t + REACH + 1) * LANES]

        width, inv_w, amount, face, edges, flux, result = {}, {}, {}, {}, {}, {}, {}
        shifted = {k: offsets == k for k in range(-SHIFT, SHIFT + 1) if k}

        def put(j):
            for f in range(5):
                v = result[j][f]
                for k, mask in shifted.items():
                    v = jnp.where(mask, result[j - k][f], v)
                columns[block, f, pl.ds(j, SUB, stride=n_steps), :] = v

        for t in range(-REACH, n_steps + REACH):
            width[t] = 1.0 + dt * tile_of(2, t)
            inv_w[t] = inverse(width[t])
            lag = tile_of(0, t) * inv_w[t]
            amount[t] = (
                lag, lag * (tile_of(3, t) - dt * tile_of(4, t)), lag * tile_of(5, t), lag * tile_of(6, t),
                lag * (tile_of(7, t) - dt * tile_of(8, t)),
            )
            if late:
                late.pop(0)()
            i = t - 2
            n = t - 3
            if n >= -1:
                us = tile_of(1, n)
                up = us > 0.0
                d = dt * us
                k1, k2, k3 = flux_weights(d, jnp.abs(d) * jnp.where(up, inv_w[n], inv_w[n + 1]))
                flux[n] = []
            face[i], edges[i] = [], []
            for f in range(5):
                if i >= -2:
                    face[i].append(face_of(*(amount[i + k][f] for k in (-1, 0, 1, 2))))
                if i >= -1:
                    edges[i].append(edges_of(amount[i][f], face[i - 1][f], face[i][f]))
                if n >= -1:
                    (low, high), (low_n, high_n) = edges[n][f], edges[n + 1][f]
                    near = jnp.where(up, high, low_n)
                    far = jnp.where(up, low, high_n)
                    mean = jnp.where(up, amount[n][f], amount[n + 1][f])
                    flux[n].append(k1 * near + k2 * mean - k3 * far)
            i = n
            if i >= 0:
                kept = [tile_of(0, i)] + [amount[i][f] * width[i] for f in range(1, 5)]
                result[i] = primitive(*(kept[f] + flux[i - 1][f] - flux[i][f] for f in range(5)))
                if i < SHIFT:
                    result[n_steps + i] = [wrapped(v, -1) for v in result[i]]
                if i >= n_steps - SHIFT:
                    result[i - n_steps] = [wrapped(v, 1) for v in result[i]]
                if i >= 2 * SHIFT:
                    put(i - SHIFT)
        for j in (n_steps - 2, n_steps - 1, 0, 1):
            late.append(lambda j=j: put(j))

    def turn(n, f, first, second):
        natural = jnp.transpose(columns[n, f])
        for k in range(n_tiles):
            for h, group in enumerate((first, second)):
                at = (k * 2 + h) * SUB
                swept[f, pl.ds((group * n_tiles + k) * SUB, SUB), :] = natural[at : at + SUB, :]

    n_own = n_rows // PAIR
    late, turns = [], []
    x_group(halo_state, 0, halo_by[...], 0, late)
    for g in range(n_own):
        x_group(state, g * SUB, rows_by[g * SUB : (g + 1) * SUB, :], g + 1, late)
        if g == 0:
            turns = [(0, f, 0, groups - 1) for f in range(5)]
        else:
            turns = [(g, f, 2 * g - 1, 2 * g) for f in range(5)]
        for args in turns:
            turn(*args)
    for put_late in late:
        put_late()
    turns = [(n_own, f, 2 * n_own - 1, 2 * n_own) for f in range(5)]

    total = groups * SUB

    def load_row(r):
        at = (r // SUB) * n_tiles * SUB + r % SUB
        rho, ta, un, tb, p = (swept[f, pl.ds(at, SUB, stride=SUB), :] for f in range(5))
        return rho, un, ta, tb, p

    oy = lines_by[...]
    moved = {k: oy == k for k in range(-SHIFT, SHIFT + 1) if k}
    cells, inv_rho, imp, faces, edges = {}, {}, {}, {}, {}
    stars, lags, weights, q_faces, q_edges, fluxes, done = {}, {}, {}, {}, {}, {}, {}
    copies, waiting = [], []
    targets = (den_out.at[0], vel_out.at[1, 0], vel_out.at[0, 0], vel_out.at[2, 0], prs_out.at[0])

    def turn_back(a, f):
        here = pl.ds(a * SUB, SUB)
        tiles = [rows_out[f, pl.ds((a * n_tiles + j) * SUB, SUB), :] for j in range(n_tiles)]
        for k, tile in enumerate(tiles):
            tiles_out[f, here, pl.ds(k * LANES, LANES)] = tile

    def send(a):
        here = pl.ds(a * SUB, SUB)
        for f in range(5):
            copies.append(
                pltpu.make_async_copy(tiles_out.at[f, here, :], targets[f].at[here, :], out_sem.at[f, a])
            )
            copies[-1].start()

    def solve_row(r):
        if turns:
            turn(*turns.pop(0))
        cells[r] = load_row(r)
        rho, un, ta, tb, p = cells[r]
        inv_rho[r] = inverse(rho)
        imp[r] = sound_impedance(rho, inv_rho[r], p)
        i = r - 2
        if i >= 1:
            faces[i] = [face_of(*(cells[i + k][f] for k in (-1, 0, 1, 2))) for f in (1, 4)]
        if i >= 2:
            edges[i] = [edges_of(cells[i][f], faces[i - 1][n], faces[i][n]) for n, f in enumerate((1, 4))]
        i = r - 3
        if i >= 2:
            (_, u_right), (_, p_right) = edges[i]
            (u_left, _), (p_left, _) = edges[i + 1]
            us, ps = riemann(imp[i], imp[i + 1], u_right, u_left, p_right, p_left)
            stars[i] = us, ps, us * ps, dt * us
        if i >= 3:
            rho, un, ta, tb, p = cells[i]
            us, ps, work, d = stars[i]
            _, ps_b, work_b, d_b = stars[i - 1]
            w = 1.0 + d - d_b
            inv_w = inverse(w)
            rate = dt * inv_rho[i]
            lag = rho * inv_w
            e = total_energy(inv_rho[i], p, un, ta, tb)
            lags[i] = (
                lag, lag * (un - rate * (ps - ps_b)), lag * ta, lag * tb, lag * (e - rate * (work - work_b)),
            )
            weights[i] = w, inv_w

    def remap_row(r):
        i = r - 5
        n = r - 6
        if n >= 5:
            d = stars[n][3]
            up = d > 0.0
            k1, k2, k3 = flux_weights(d, jnp.abs(d) * jnp.where(up, weights[n][1], weights[n + 1][1]))
            fluxes[n] = []
        q_faces[i], q_edges[i] = [], []
        for f in range(5):
            if i >= 4:
                q_faces[i].append(face_of(*(lags[i + k][f] for k in (-1, 0, 1, 2))))
            if i >= 5:
                q_edges[i].append(edges_of(lags[i][f], q_faces[i - 1][f], q_faces[i][f]))
            if n >= 5:
                (low, high), (low_n, high_n) = q_edges[n][f], q_edges[n + 1][f]
                near = jnp.where(up, high, low_n)
                far = jnp.where(up, low, high_n)
                fluxes[n].append(k1 * near + k2 * jnp.where(up, lags[n][f], lags[n + 1][f]) - k3 * far)
        i = n
        if i >= 6:
            done[i] = primitive(
                *(lags[i][f] * weights[i][0] + fluxes[i - 1][f] - fluxes[i][f] for f in range(5))
            )
        i = r - 8
        if i >= HALO:
            j = i - HALO
            a, b = divmod(j, SUB)
            for f in range(5):
                v = done[i][f]
                for k, mask in moved.items():
                    v = jnp.where(mask, done[i - k][f], v)
                rows_out[f, pl.ds(a * n_tiles * SUB + b, SUB, stride=SUB), :] = v
            if b == SUB - 1:
                if a:
                    send(a - 1)
                waiting.extend((a, f) for f in range(5))
        if waiting:
            turn_back(*waiting.pop(0))

    for r in range(total + LEAD):
        if r < total:
            solve_row(r)
        if r >= LEAD:
            remap_row(r - LEAD)
    for a, f in waiting:
        turn_back(a, f)
    send(n_rows // SUB - 1)
    for copy in copies:
        copy.wait()


def body(n_dev, n_cols, density, velocity, pressure, offsets_x, offsets_y):
    n_rows, n_x = density.shape[1:]
    f32 = jnp.float32
    vmem = pl.BlockSpec(memory_space=pltpu.VMEM)
    everyone = n_dev * n_cols
    small = pltpu.CompilerParams(vmem_limit_bytes=16 * 2**20)
    hbm = pl.BlockSpec(memory_space=pltpu.HBM)
    wide = 5 * n_x + LANES
    halo = jax.ShapeDtypeStruct((HALO, wide), f32)
    pay, up, down = pl.pallas_call(
        speed_kernel,
        out_shape=(jax.ShapeDtypeStruct((everyone, LANES), f32), halo, halo),
        in_specs=[hbm] * 4,
        out_specs=[hbm] * 3,
        scratch_shapes=[
            pltpu.VMEM((everyone, LANES), f32),
            pltpu.VMEM((n_rows, wide), f32),
            pltpu.VMEM(offsets_x.shape, jnp.int32),
            pltpu.VMEM((1, LANES), f32),
            pltpu.SemaphoreType.DMA((6,)),
            pltpu.SemaphoreType.DMA((3,)),
        ],
        compiler_params=pltpu.CompilerParams(vmem_limit_bytes=A_LIMIT),
    )(density, velocity, pressure, offsets_x)
    got = lax.all_to_all(pay, ("rows", "cols"), split_axis=0, concat_axis=0, tiled=True)
    before = lax.ppermute(up, "rows", [(i, (i + 1) % n_dev) for i in range(n_dev)])
    after = lax.ppermute(down, "rows", [(i, (i - 1) % n_dev) for i in range(n_dev)])
    long = (LANES // SUB + 2 * REACH) * LANES
    rooms = pltpu.VMEM((5, LANES, LANES), f32)
    n_own = n_rows // PAIR
    state, rows_by, lines_by = pl.pallas_call(
        own_kernel,
        out_shape=(
            jax.ShapeDtypeStruct((9, n_own * SUB, long), f32),
            jax.ShapeDtypeStruct((n_own * SUB, LANES), f32),
            jax.ShapeDtypeStruct((SUB, LANES), f32),
        ),
        in_specs=[vmem] * 5,
        out_specs=[vmem] * 3,
        scratch_shapes=[pltpu.VMEM((1, LANES), f32), pltpu.VMEM((n_own, 5, LANES, LANES), f32)],
        compiler_params=small,
        cost_estimate=pl.CostEstimate(flops=OWN_COST, bytes_accessed=10**6, transcendentals=0),
    )(density, velocity, pressure, offsets_x, offsets_y)
    halo_state, halo_by = pl.pallas_call(
        halo_kernel,
        out_shape=(
            jax.ShapeDtypeStruct((9, SUB, long), f32), jax.ShapeDtypeStruct((SUB, LANES), f32),
        ),
        in_specs=[vmem] * 2,
        out_specs=[vmem] * 2,
        scratch_shapes=[rooms],
        compiler_params=small,
        cost_estimate=pl.CostEstimate(flops=HALO_COST, bytes_accessed=10**6, transcendentals=0),
    )(before, after)
    plane = jax.ShapeDtypeStruct(density.shape, f32)
    tall = (n_rows + 2 * HALO) * n_x // LANES
    short = n_rows * n_x // LANES
    return pl.pallas_call(
        sweep_kernel,
        out_shape=(plane, jax.ShapeDtypeStruct(velocity.shape, f32), plane),
        in_specs=[vmem] * 6,
        out_specs=[hbm] * 3,
        scratch_shapes=[
            pltpu.VMEM((n_own + 1, 5, LANES, LANES), f32),
            pltpu.VMEM((5, tall, LANES), f32),
            pltpu.VMEM((5, short, LANES), f32),
            pltpu.VMEM((5, n_rows, n_x), f32),
            pltpu.SemaphoreType.DMA((5, n_rows // SUB)),
        ],
        compiler_params=small,
    )(state, halo_state, got, rows_by, halo_by, lines_by)


def solution(mesh):
    n_dev, n_cols = mesh.shape["rows"], mesh.shape["cols"]
    return jax.shard_map(
        lambda *arrays: body(n_dev, n_cols, *arrays),
        mesh=mesh,
        in_specs=(
            P("cols", "rows", None),
            P(None, "cols", "rows", None),
            P("cols", "rows", None),
            P("cols", "rows"),
            P("cols", None),
        ),
        out_specs=(P("cols", "rows", None), P(None, "cols", "rows", None), P("cols", "rows", None)),
        check_vma=False,
    )
```

```python
import jax
import jax.numpy as jnp
from jax import lax
from jax.experimental import pallas as pl
from jax.experimental.pallas import tpu as pltpu
from jax.sharding import PartitionSpec as P

SHIFT = 2
PAIR = 16
REACH = 2
A_LIMIT = 60 * 2**20
OWN_COST = 10**6
HALO_COST = 10**6
LEAD = 10
HALO = 8
LANES = 128
SUB = 8

courant = 0.4
adiabatic = 5.0 / 3.0


def inverse(v):
    return 1.0 / v


def clamp(v, a, b):
    return jnp.minimum(jnp.maximum(v, jnp.minimum(a, b)), jnp.maximum(a, b))


def face_of(am, a0, a1, a2):
    face = 7.0 / 12.0 * (a0 + a1) - 1.0 / 12.0 * (am + a2)
    return clamp(face, a0, a1)


def edges_of(a, face_before, face):
    triple = 3.0 * a
    low = clamp(face_before, a, triple - 2.0 * face)
    high = clamp(face, a, triple - 2.0 * face_before)
    return low, high


def sound_impedance(rho, inv_rho, p):
    return rho * jnp.sqrt(adiabatic * p * inv_rho)


def riemann(z, zn, u_right, u_left, p_right, p_left):
    inv = inverse(z + zn)
    us = (z * u_right + zn * u_left + p_right - p_left) * inv
    ps = (zn * p_right + z * p_left + z * zn * (u_right - u_left)) * inv
    return us, ps


def total_energy(inv_rho, p, un, ta, tb):
    return p * inv_rho * (1.0 / (adiabatic - 1.0)) + 0.5 * (un * un + ta * ta + tb * tb)


def flux_weights(d, f):
    rest = 1.0 - f
    near = d * rest
    return near * rest, f * near


def gaps_of(gap, step, gap_before, step_before):
    left = gap_before - step_before
    return clamp(left, 0.0, -2.0 * gap), clamp(gap, 0.0, -2.0 * left)


def step_and_gap(before, a, after, after2):
    step = after - a
    gap = 0.5 * step + (1.0 / 12.0) * ((a - before) - (after2 - after))
    return step, clamp(gap, 0.0, step)


def flux_of(up, d, k_near, k_far, a, gaps, a_next, gaps_next):
    (low, high), (low_next, high_next) = gaps, gaps_next
    near = jnp.where(up, high, low_next)
    far = jnp.where(up, low, high_next)
    return d * jnp.where(up, a, a_next) + k_near * near - k_far * far


def primitive(mass, mn, ma, mb, energy):
    inv = inverse(mass)
    kinetic = 0.5 * (mn * mn + ma * ma + mb * mb) * inv
    return mass, mn * inv, ma * inv, mb * inv, (adiabatic - 1.0) * (energy - kinetic)


def split(v):
    return [v[:, k : k + LANES] for k in range(0, v.shape[1], LANES)]


def to_columns(halves, room):
    rows = [half[:, k : k + LANES] for k in range(0, halves[0].shape[1], LANES) for half in halves]
    room[...] = jnp.transpose(jnp.concatenate(rows, axis=0))
    return [room[pl.ds(j, SUB, stride=LANES // SUB), :] for j in range(LANES // SUB)]


def wrapped(tile, way):
    sub = lax.broadcasted_iota(jnp.int32, tile.shape, 0)
    turned = pltpu.roll(tile, way % SUB, 0)
    edge = 0 if way > 0 else SUB - 1
    return jnp.where(sub == edge, pltpu.roll(turned, way * PAIR % LANES, 1), turned)


def roll_x(v, k):
    parts = split(v)
    n = len(parts)
    moved = []
    for j in range(n):
        turns, source = divmod(j - k, n)
        moved.append(parts[source] if turns == 0 else wrapped(parts[source], -turns))
    return jnp.concatenate(moved, axis=1)


def profile_x(a):
    nxt = roll_x(a, -1)
    face = face_of(roll_x(a, 1), a, nxt, roll_x(a, -2))
    low, high = edges_of(a, roll_x(face, 1), face)
    return nxt, low, high


def lines_of(offx, first):
    shape = (SUB, LANES)
    lane = lax.broadcasted_iota(jnp.int32, shape, 1)
    row = lax.broadcasted_iota(jnp.int32, shape, 0)
    found = jnp.where(lane == row + first, jnp.broadcast_to(offx, shape), 0.0)
    return jnp.broadcast_to(jnp.sum(found, axis=1, keepdims=True), shape)


def speed_kernel(den, vel, prs, offx_hbm, pay_hbm, up, down, pay, block, offx, line, sems, pack_sems):
    n_rows, n_x = den.shape[1:]
    off_load = pltpu.make_async_copy(offx_hbm, offx, sems.at[5])
    sources = (den.at[0], vel.at[0, 0], vel.at[1, 0], vel.at[2, 0], prs.at[0])
    loads = [pltpu.make_async_copy(sources[f], block.at[:, pl.ds(f * n_x, n_x)], sems.at[f]) for f in range(5)]
    for load in (*loads, off_load):
        load.start()
    line[...] = jnp.zeros_like(line)
    off_load.wait()
    line[:, 0:n_rows] = offx[...].astype(jnp.float32)
    for first in (0, n_rows - HALO):
        block[first : first + HALO, 5 * n_x :] = lines_of(line[...], first)
    for load in loads:
        load.wait()
    packs = [
        pltpu.make_async_copy(block.at[pl.ds(first, HALO), :], out, pack_sems.at[k])
        for k, (out, first) in enumerate(((up, n_rows - HALO), (down, 0)))
    ]
    for pack in packs:
        pack.start()
    peak = None
    for g in range(n_rows // SUB):
        rho, un, ta, p = (block[g * SUB : (g + 1) * SUB, f * n_x : (f + 1) * n_x] for f in (0, 1, 2, 4))
        s = jnp.maximum(jnp.abs(un), jnp.abs(ta)) + jnp.sqrt(adiabatic * p / rho)
        peak = s if peak is None else jnp.maximum(peak, s)
    tiles = split(peak)
    while len(tiles) > 1:
        tiles = [jnp.maximum(x, y) for x, y in zip(tiles[::2], tiles[1::2])]
    top = jnp.max(jnp.max(tiles[0], axis=0, keepdims=True), axis=1, keepdims=True)
    pay[...] = jnp.broadcast_to(top, pay.shape)
    packs.append(pltpu.make_async_copy(pay, pay_hbm, pack_sems.at[2]))
    packs[-1].start()
    for pack in packs:
        pack.wait()


def prepare(halves, state, row, by, rooms):
    rho, un, ta, tb, p = (
        jnp.concatenate(to_columns([h[f] for h in halves], rooms.at[f]), axis=1) for f in range(5)
    )
    lines = jnp.concatenate([h[5] for h in halves] * (LANES // PAIR), axis=0)
    by[pl.ds(row, SUB), :] = jnp.transpose(lines)[0:SUB, :]
    inv = inverse(rho)
    z = sound_impedance(rho, inv, p)
    _, u_low, u_high = profile_x(un)
    _, p_low, p_high = profile_x(p)
    us, ps = riemann(z, roll_x(z, -1), u_high, roll_x(u_low, -1), p_high, roll_x(p_low, -1))
    work = us * ps
    o = pl.ds(row, SUB)
    values = (
        rho, us, us - roll_x(us, 1), un, (ps - roll_x(ps, 1)) * inv, ta, tb,
        total_energy(inv, p, un, ta, tb), (work - roll_x(work, 1)) * inv,
    )
    for n, v in enumerate(values):
        tiles = split(v)
        ends = [wrapped(t, 1) for t in tiles[-REACH:]], [wrapped(t, -1) for t in tiles[:REACH]]
        for t, tile in enumerate(ends[0] + tiles + ends[1]):
            state[n, o, t * LANES : (t + 1) * LANES] = tile


def own_kernel(den, vel, prs, offx, offy, state, rows_by, lines_by, line, rooms):
    n_rows, n_x = den.shape[1:]
    for k in range(n_x // LANES):
        lines_by[k : k + 1, :] = offy[:, k * LANES : (k + 1) * LANES].astype(jnp.float32)
    line[...] = jnp.zeros_like(line)
    line[:, 0:n_rows] = offx[...].astype(jnp.float32)
    for g in range(n_rows // PAIR):
        halves = []
        for first in range(g * PAIR, (g + 1) * PAIR, SUB):
            r = pl.ds(first, SUB)
            halves.append(
                [den[0, r, :], vel[0, 0, r, :], vel[1, 0, r, :], vel[2, 0, r, :], prs[0, r, :], lines_of(line[...], first)]
            )
        prepare(halves, state, g * SUB, rows_by, rooms.at[g])


def halo_kernel(before, after, state, rows_by, rooms):
    n_x = (before.shape[1] - LANES) // 5
    halves = [[ref[:, f * n_x : (f + 1) * n_x] for f in range(5)] + [ref[:, 5 * n_x :]] for ref in (before, after)]
    prepare(halves, state, 0, rows_by, rooms)


def sweep_kernel(
    state, halo_state, got, rows_by, halo_by, lines_by, den_out, vel_out, prs_out,
    columns, swept, rows_out, tiles_out, out_sem,
):
    n_rows, n_x = den_out.shape[1:]
    n_tiles = n_x // LANES
    groups = n_rows // SUB + 2
    n_steps = LANES // SUB
    top = [got[k * SUB : (k + 1) * SUB, :] for k in range(got.shape[0] // SUB)]
    while len(top) > 1:
        top = [jnp.maximum(x, y) for x, y in zip(top[::2], top[1::2])]
    dt = courant / jnp.max(top[0], axis=0, keepdims=True)

    def x_group(state, row, offsets, block, late):
        o = pl.ds(row, SUB)

        def tile_of(n, t):
            return state[n, o, (t + REACH) * LANES : (t + REACH + 1) * LANES]

        width, inv_w, amount, step, face, gaps, flux, result = {}, {}, {}, {}, {}, {}, {}, {}
        bits = offsets + float(SHIFT)
        high_bit = bits > 3.5
        low_bits = jnp.where(high_bit, 0.0, bits)
        mid_bit = low_bits > 1.5
        odd = low_bits - jnp.where(mid_bit, 2.0, 0.0) > 0.5
        once = {}

        def moved_one(j, f):
            if (j, f) not in once:
                once[j, f] = jnp.where(odd, result[j - 1][f], result[j][f])
            return once[j, f]

        def put(j):
            for f in range(5):
                v = jnp.where(mid_bit, moved_one(j, f), moved_one(j + 2, f))
                v = jnp.where(high_bit, result[j - 2][f], v)
                columns[block, f, pl.ds(j, SUB, stride=n_steps), :] = v

        def finish(i):
            kept = [tile_of(0, i)] + [amount[i][f] * width[i] for f in range(1, 5)]
            result[i] = primitive(*(kept[f] + flux[i - 1][f] - flux[i][f] for f in range(5)))
            if i < SHIFT:
                result[n_steps + i] = [wrapped(v, -1) for v in result[i]]
            if i >= n_steps - SHIFT:
                result[i - n_steps] = [wrapped(v, 1) for v in result[i]]

        def first():
            flux[-1] = [wrapped(v, 1) for v in flux[n_steps - 1]]
            finish(0)

        for t in range(-REACH, n_steps + 3):
            if t < n_steps + REACH:
                width[t] = 1.0 + dt * tile_of(2, t)
                inv_w[t] = inverse(width[t])
                lag = tile_of(0, t) * inv_w[t]
                amount[t] = (
                    lag, lag * (tile_of(3, t) - dt * tile_of(4, t)), lag * tile_of(5, t), lag * tile_of(6, t),
                    lag * (tile_of(7, t) - dt * tile_of(8, t)),
                )
            if late:
                late.pop(0)()
            i = t - 2
            c = t - 3
            if c >= 0:
                us = tile_of(1, c)
                up = us > 0.0
                d = dt * us
                weights = flux_weights(d, jnp.abs(d) * jnp.where(up, inv_w[c], inv_w[c + 1]))
                flux[c] = []
            step[i], face[i], gaps[i] = [], [], []
            for f in range(5):
                if -1 <= i < n_steps:
                    steps = step_and_gap(*(amount[i + k][f] for k in (-1, 0, 1, 2)))
                    step[i].append(steps[0])
                    face[i].append(steps[1])
                if 0 <= i < n_steps:
                    gaps[i].append(gaps_of(face[i][f], step[i][f], face[i - 1][f], step[i - 1][f]))
                if i == n_steps:
                    gaps[i].append([wrapped(v, -1) for v in gaps[0][f]])
                if c >= 0:
                    flux[c].append(flux_of(up, d, *weights, amount[c][f], gaps[c][f], amount[c + 1][f], gaps[c + 1][f]))
            if c >= 1:
                finish(c)
                if c >= 2 * SHIFT + 1:
                    put(c - SHIFT)
        late.append(first)
        for j in (n_steps - 2, n_steps - 1, 0, 1, 2):
            late.append(lambda j=j: put(j))

    def turn(n, f, first, second):
        natural = jnp.transpose(columns[n, f])
        for k in range(n_tiles):
            for h, group in enumerate((first, second)):
                at = (k * 2 + h) * SUB
                swept[f, pl.ds((group * n_tiles + k) * SUB, SUB), :] = natural[at : at + SUB, :]

    n_own = n_rows // PAIR
    late, turns = [], []
    x_group(halo_state, 0, halo_by[...], 0, late)
    for g in range(n_own):
        x_group(state, g * SUB, rows_by[g * SUB : (g + 1) * SUB, :], g + 1, late)
        if g == 0:
            turns = [(0, f, 0, groups - 1) for f in range(5)]
        else:
            turns = [(g, f, 2 * g - 1, 2 * g) for f in range(5)]
        for args in turns:
            turn(*args)
    for put_late in late:
        put_late()
    turns = [(n_own, f, 2 * n_own - 1, 2 * n_own) for f in range(5)]

    total = groups * SUB

    def load_row(r):
        at = (r // SUB) * n_tiles * SUB + r % SUB
        rho, ta, un, tb, p = (swept[f, pl.ds(at, SUB, stride=SUB), :] for f in range(5))
        return rho, un, ta, tb, p

    bits = lines_by[...] + float(SHIFT)
    high_bit = bits > 3.5
    low_bits = jnp.where(high_bit, 0.0, bits)
    mid_bit = low_bits > 1.5
    odd = low_bits - jnp.where(mid_bit, 2.0, 0.0) > 0.5
    once = {}

    def moved_one(i, f):
        if (i, f) not in once:
            once[i, f] = jnp.where(odd, done[i - 1][f], done[i][f])
        return once[i, f]

    cells, inv_rho, imp, faces, edges = {}, {}, {}, {}, {}
    stars, lags, weights, q_steps, q_faces, q_edges, fluxes, done = {}, {}, {}, {}, {}, {}, {}, {}
    copies, waiting = [], []
    targets = (den_out.at[0], vel_out.at[1, 0], vel_out.at[0, 0], vel_out.at[2, 0], prs_out.at[0])

    def turn_back(a, f):
        here = pl.ds(a * SUB, SUB)
        tiles = [rows_out[f, pl.ds((a * n_tiles + j) * SUB, SUB), :] for j in range(n_tiles)]
        for k, tile in enumerate(tiles):
            tiles_out[f, here, pl.ds(k * LANES, LANES)] = tile

    def send(a, f):
        here = pl.ds(a * SUB, SUB)
        copies.append(pltpu.make_async_copy(tiles_out.at[f, here, :], targets[f].at[here, :], out_sem.at[f, a]))
        copies[-1].start()

    def solve_row(r):
        if turns:
            turn(*turns.pop(0))
        cells[r] = load_row(r)
        rho, un, ta, tb, p = cells[r]
        inv_rho[r] = inverse(rho)
        imp[r] = sound_impedance(rho, inv_rho[r], p)
        i = r - 2
        if i >= 1:
            faces[i] = [face_of(*(cells[i + k][f] for k in (-1, 0, 1, 2))) for f in (1, 4)]
        if i >= 2:
            edges[i] = [edges_of(cells[i][f], faces[i - 1][n], faces[i][n]) for n, f in enumerate((1, 4))]
        i = r - 3
        if i >= 2:
            (_, u_right), (_, p_right) = edges[i]
            (u_left, _), (p_left, _) = edges[i + 1]
            us, ps = riemann(imp[i], imp[i + 1], u_right, u_left, p_right, p_left)
            stars[i] = us, ps, us * ps, dt * us
        if i >= 3:
            rho, un, ta, tb, p = cells[i]
            us, ps, work, d = stars[i]
            _, ps_b, work_b, d_b = stars[i - 1]
            w = 1.0 + d - d_b
            inv_w = inverse(w)
            rate = dt * inv_rho[i]
            lag = rho * inv_w
            e = total_energy(inv_rho[i], p, un, ta, tb)
            lags[i] = (
                lag, lag * (un - rate * (ps - ps_b)), lag * ta, lag * tb, lag * (e - rate * (work - work_b)),
            )
            weights[i] = w, inv_w

    def remap_row(r):
        i = r - 5
        n = r - 6
        if n >= 5:
            d = stars[n][3]
            up = d > 0.0
            near_far = flux_weights(d, jnp.abs(d) * jnp.where(up, weights[n][1], weights[n + 1][1]))
            fluxes[n] = []
        q_steps[i], q_faces[i], q_edges[i] = [], [], []
        for f in range(5):
            if i >= 4:
                step, face = step_and_gap(*(lags[i + k][f] for k in (-1, 0, 1, 2)))
                q_steps[i].append(step)
                q_faces[i].append(face)
            if i >= 5:
                q_edges[i].append(gaps_of(q_faces[i][f], q_steps[i][f], q_faces[i - 1][f], q_steps[i - 1][f]))
            if n >= 5:
                fluxes[n].append(
                    flux_of(up, d, *near_far, lags[n][f], q_edges[n][f], lags[n + 1][f], q_edges[n + 1][f])
                )
        i = n
        if i >= 6:
            done[i] = primitive(
                *(
                    (lags[i][f] * weights[i][0] if f else cells[i][0]) + fluxes[i - 1][f] - fluxes[i][f]
                    for f in range(5)
                )
            )
        i = r - 8
        if i >= HALO:
            j = i - HALO
            a, b = divmod(j, SUB)
            for f in range(5):
                v = jnp.where(mid_bit, moved_one(i, f), moved_one(i + 2, f))
                v = jnp.where(high_bit, done[i - 2][f], v)
                rows_out[f, pl.ds(a * n_tiles * SUB + b, SUB, stride=SUB), :] = v
            if b == SUB - 1:
                if a:
                    for f in range(5):
                        send(a - 1, f)
                waiting.extend((a, f) for f in range(5))
        if waiting:
            turn_back(*waiting.pop(0))

    for r in range(total + LEAD):
        if r < total:
            solve_row(r)
        if r >= LEAD:
            remap_row(r - LEAD)
    for f in range(5):
        if (n_rows // SUB - 1, f) in waiting:
            turn_back(n_rows // SUB - 1, f)
        send(n_rows // SUB - 1, f)
    for copy in copies:
        copy.wait()


def body(n_dev, n_cols, density, velocity, pressure, offsets_x, offsets_y):
    n_rows, n_x = density.shape[1:]
    f32 = jnp.float32
    vmem = pl.BlockSpec(memory_space=pltpu.VMEM)
    everyone = n_dev * n_cols
    small = pltpu.CompilerParams(vmem_limit_bytes=16 * 2**20)
    hbm = pl.BlockSpec(memory_space=pltpu.HBM)
    wide = 5 * n_x + LANES
    halo = jax.ShapeDtypeStruct((HALO, wide), f32)
    pay, up, down = pl.pallas_call(
        speed_kernel,
        out_shape=(jax.ShapeDtypeStruct((everyone, LANES), f32), halo, halo),
        in_specs=[hbm] * 4,
        out_specs=[hbm] * 3,
        scratch_shapes=[
            pltpu.VMEM((everyone, LANES), f32),
            pltpu.VMEM((n_rows, wide), f32),
            pltpu.VMEM(offsets_x.shape, jnp.int32),
            pltpu.VMEM((1, LANES), f32),
            pltpu.SemaphoreType.DMA((6,)),
            pltpu.SemaphoreType.DMA((3,)),
        ],
        compiler_params=pltpu.CompilerParams(vmem_limit_bytes=A_LIMIT),
    )(density, velocity, pressure, offsets_x)
    got = lax.all_to_all(pay, ("rows", "cols"), split_axis=0, concat_axis=0, tiled=True)
    before = lax.ppermute(up, "rows", [(i, (i + 1) % n_dev) for i in range(n_dev)])
    after = lax.ppermute(down, "rows", [(i, (i - 1) % n_dev) for i in range(n_dev)])
    long = (LANES // SUB + 2 * REACH) * LANES
    rooms = pltpu.VMEM((5, LANES, LANES), f32)
    n_own = n_rows // PAIR
    state, rows_by, lines_by = pl.pallas_call(
        own_kernel,
        out_shape=(
            jax.ShapeDtypeStruct((9, n_own * SUB, long), f32),
            jax.ShapeDtypeStruct((n_own * SUB, LANES), f32),
            jax.ShapeDtypeStruct((SUB, LANES), f32),
        ),
        in_specs=[vmem] * 5,
        out_specs=[vmem] * 3,
        scratch_shapes=[pltpu.VMEM((1, LANES), f32), pltpu.VMEM((n_own, 5, LANES, LANES), f32)],
        compiler_params=small,
        cost_estimate=pl.CostEstimate(flops=OWN_COST, bytes_accessed=10**6, transcendentals=0),
    )(density, velocity, pressure, offsets_x, offsets_y)
    halo_state, halo_by = pl.pallas_call(
        halo_kernel,
        out_shape=(
            jax.ShapeDtypeStruct((9, SUB, long), f32), jax.ShapeDtypeStruct((SUB, LANES), f32),
        ),
        in_specs=[vmem] * 2,
        out_specs=[vmem] * 2,
        scratch_shapes=[rooms],
        compiler_params=small,
        cost_estimate=pl.CostEstimate(flops=HALO_COST, bytes_accessed=10**6, transcendentals=0),
    )(before, after)
    plane = jax.ShapeDtypeStruct(density.shape, f32)
    tall = (n_rows + 2 * HALO) * n_x // LANES
    short = n_rows * n_x // LANES
    return pl.pallas_call(
        sweep_kernel,
        out_shape=(plane, jax.ShapeDtypeStruct(velocity.shape, f32), plane),
        in_specs=[vmem] * 6,
        out_specs=[hbm] * 3,
        scratch_shapes=[
            pltpu.VMEM((n_own + 1, 5, LANES, LANES), f32),
            pltpu.VMEM((5, tall, LANES), f32),
            pltpu.VMEM((5, short, LANES), f32),
            pltpu.VMEM((5, n_rows, n_x), f32),
            pltpu.SemaphoreType.DMA((5, n_rows // SUB)),
        ],
        compiler_params=small,
    )(state, halo_state, got, rows_by, halo_by, lines_by)


def solution(mesh):
    n_dev, n_cols = mesh.shape["rows"], mesh.shape["cols"]
    return jax.shard_map(
        lambda *arrays: body(n_dev, n_cols, *arrays),
        mesh=mesh,
        in_specs=(
            P("cols", "rows", None),
            P(None, "cols", "rows", None),
            P("cols", "rows", None),
            P("cols", "rows"),
            P("cols", None),
        ),
        out_specs=(P("cols", "rows", None), P(None, "cols", "rows", None), P("cols", "rows", None)),
        check_vma=False,
    )
```

```python
import jax
import jax.numpy as jnp
from jax import lax
from jax.experimental import pallas as pl
from jax.experimental.pallas import tpu as pltpu
from jax.sharding import PartitionSpec as P

SHIFT = 2
PAIR = 16
REACH = 2
A_LIMIT = 60 * 2**20
OWN_COST = 10**6
HALO_COST = 10**6
LEAD = 10
HALO = 8
LANES = 128
SUB = 8

courant = 0.4
adiabatic = 5.0 / 3.0


def inverse(v):
    return 1.0 / v


def clamp(v, a, b):
    return jnp.minimum(jnp.maximum(v, jnp.minimum(a, b)), jnp.maximum(a, b))


def face_of(am, a0, a1, a2):
    face = 7.0 / 12.0 * (a0 + a1) - 1.0 / 12.0 * (am + a2)
    return clamp(face, a0, a1)


def edges_of(a, face_before, face):
    triple = 3.0 * a
    low = clamp(face_before, a, triple - 2.0 * face)
    high = clamp(face, a, triple - 2.0 * face_before)
    return low, high


def sound_impedance(rho, inv_rho, p):
    return rho * jnp.sqrt(adiabatic * p * inv_rho)


def riemann(z, zn, u_right, u_left, p_right, p_left):
    inv = inverse(z + zn)
    us = (z * u_right + zn * u_left + p_right - p_left) * inv
    ps = (zn * p_right + z * p_left + z * zn * (u_right - u_left)) * inv
    return us, ps


def total_energy(inv_rho, p, un, ta, tb):
    return p * inv_rho * (1.0 / (adiabatic - 1.0)) + 0.5 * (un * un + ta * ta + tb * tb)


def flux_weights(d, f):
    rest = 1.0 - f
    near = d * rest
    return near * rest, f * near


def gaps_of(gap, step, gap_before, step_before):
    left = gap_before - step_before
    return clamp(left, 0.0, -2.0 * gap), clamp(gap, 0.0, -2.0 * left)


def step_and_gap(before, a, after, after2):
    step = after - a
    gap = 0.5 * step + (1.0 / 12.0) * ((a - before) - (after2 - after))
    return step, clamp(gap, 0.0, step)


def flux_of(up, d, k_near, k_far, a, gaps, a_next, gaps_next):
    (low, high), (low_next, high_next) = gaps, gaps_next
    near = jnp.where(up, high, low_next)
    far = jnp.where(up, low, high_next)
    return d * jnp.where(up, a, a_next) + k_near * near - k_far * far


def primitive(mass, mn, ma, mb, energy):
    inv = inverse(mass)
    kinetic = 0.5 * (mn * mn + ma * ma + mb * mb) * inv
    return mass, mn * inv, ma * inv, mb * inv, (adiabatic - 1.0) * (energy - kinetic)


def split(v):
    return [v[:, k : k + LANES] for k in range(0, v.shape[1], LANES)]


def to_columns(halves, room):
    rows = [half[:, k : k + LANES] for k in range(0, halves[0].shape[1], LANES) for half in halves]
    room[...] = jnp.transpose(jnp.concatenate(rows, axis=0))
    return [room[pl.ds(j, SUB, stride=LANES // SUB), :] for j in range(LANES // SUB)]


def wrapped(tile, way):
    sub = lax.broadcasted_iota(jnp.int32, tile.shape, 0)
    turned = pltpu.roll(tile, way % SUB, 0)
    edge = 0 if way > 0 else SUB - 1
    return jnp.where(sub == edge, pltpu.roll(turned, way * PAIR % LANES, 1), turned)


def roll_x(v, k):
    parts = split(v)
    n = len(parts)
    moved = []
    for j in range(n):
        turns, source = divmod(j - k, n)
        moved.append(parts[source] if turns == 0 else wrapped(parts[source], -turns))
    return jnp.concatenate(moved, axis=1)


def profile_x(a):
    nxt = roll_x(a, -1)
    face = face_of(roll_x(a, 1), a, nxt, roll_x(a, -2))
    low, high = edges_of(a, roll_x(face, 1), face)
    return nxt, low, high


def lines_of(offx, first):
    shape = (SUB, LANES)
    lane = lax.broadcasted_iota(jnp.int32, shape, 1)
    row = lax.broadcasted_iota(jnp.int32, shape, 0)
    found = jnp.where(lane == row + first, jnp.broadcast_to(offx, shape), 0.0)
    return jnp.broadcast_to(jnp.sum(found, axis=1, keepdims=True), shape)


def speed_kernel(den, vel, prs, offx_hbm, pay_hbm, up, down, pay, block, offx, line, sems, pack_sems):
    n_rows, n_x = den.shape[1:]
    off_load = pltpu.make_async_copy(offx_hbm, offx, sems.at[5])
    sources = (den.at[0], vel.at[0, 0], vel.at[1, 0], vel.at[2, 0], prs.at[0])
    loads = [pltpu.make_async_copy(sources[f], block.at[:, pl.ds(f * n_x, n_x)], sems.at[f]) for f in (4, 0, 1, 2)]
    for first, sem in ((0, 3), (n_rows - HALO, 6)):
        rows = pl.ds(first, HALO)
        loads.append(
            pltpu.make_async_copy(sources[3].at[rows, :], block.at[rows, pl.ds(3 * n_x, n_x)], sems.at[sem])
        )
    for load in (*loads, off_load):
        load.start()
    line[...] = jnp.zeros_like(line)
    off_load.wait()
    line[:, 0:n_rows] = offx[...].astype(jnp.float32)
    for first in (0, n_rows - HALO):
        block[first : first + HALO, 5 * n_x :] = lines_of(line[...], first)
    for load in loads:
        load.wait()
    packs = [
        pltpu.make_async_copy(block.at[pl.ds(first, HALO), :], out, pack_sems.at[k])
        for k, (out, first) in enumerate(((up, n_rows - HALO), (down, 0)))
    ]
    for pack in packs:
        pack.start()
    peak = None
    for g in range(n_rows // SUB):
        rho, un, ta, p = (block[g * SUB : (g + 1) * SUB, f * n_x : (f + 1) * n_x] for f in (0, 1, 2, 4))
        s = jnp.maximum(jnp.abs(un), jnp.abs(ta)) + jnp.sqrt(adiabatic * p / rho)
        peak = s if peak is None else jnp.maximum(peak, s)
    tiles = split(peak)
    while len(tiles) > 1:
        tiles = [jnp.maximum(x, y) for x, y in zip(tiles[::2], tiles[1::2])]
    top = jnp.max(jnp.max(tiles[0], axis=0, keepdims=True), axis=1, keepdims=True)
    pay[...] = jnp.broadcast_to(top, pay.shape)
    packs.append(pltpu.make_async_copy(pay, pay_hbm, pack_sems.at[2]))
    packs[-1].start()
    for pack in packs:
        pack.wait()


def prepare(halves, state, row, by, rooms):
    rho, un, ta, tb, p = (
        jnp.concatenate(to_columns([h[f] for h in halves], rooms.at[f]), axis=1) for f in range(5)
    )
    lines = jnp.concatenate([h[5] for h in halves] * (LANES // PAIR), axis=0)
    by[pl.ds(row, SUB), :] = jnp.transpose(lines)[0:SUB, :]
    inv = inverse(rho)
    z = sound_impedance(rho, inv, p)
    _, u_low, u_high = profile_x(un)
    _, p_low, p_high = profile_x(p)
    us, ps = riemann(z, roll_x(z, -1), u_high, roll_x(u_low, -1), p_high, roll_x(p_low, -1))
    work = us * ps
    o = pl.ds(row, SUB)
    values = (
        rho, us, us - roll_x(us, 1), un, (ps - roll_x(ps, 1)) * inv, ta, tb,
        total_energy(inv, p, un, ta, tb), (work - roll_x(work, 1)) * inv,
    )
    for n, v in enumerate(values):
        tiles = split(v)
        ends = [wrapped(t, 1) for t in tiles[-REACH:]], [wrapped(t, -1) for t in tiles[:REACH]]
        for t, tile in enumerate(ends[0] + tiles + ends[1]):
            state[n, o, t * LANES : (t + 1) * LANES] = tile


def own_kernel(den, vel, prs, offx, offy, state, rows_by, lines_by, line, rooms):
    n_rows, n_x = den.shape[1:]
    for k in range(n_x // LANES):
        lines_by[k : k + 1, :] = offy[:, k * LANES : (k + 1) * LANES].astype(jnp.float32)
    line[...] = jnp.zeros_like(line)
    line[:, 0:n_rows] = offx[...].astype(jnp.float32)
    for g in range(n_rows // PAIR):
        halves = []
        for first in range(g * PAIR, (g + 1) * PAIR, SUB):
            r = pl.ds(first, SUB)
            halves.append(
                [den[0, r, :], vel[0, 0, r, :], vel[1, 0, r, :], vel[2, 0, r, :], prs[0, r, :], lines_of(line[...], first)]
            )
        prepare(halves, state, g * SUB, rows_by, rooms.at[g])


def halo_kernel(before, after, state, rows_by, rooms):
    n_x = (before.shape[1] - LANES) // 5
    halves = [[ref[:, f * n_x : (f + 1) * n_x] for f in range(5)] + [ref[:, 5 * n_x :]] for ref in (before, after)]
    prepare(halves, state, 0, rows_by, rooms)


def sweep_kernel(
    state, halo_state, got, rows_by, halo_by, lines_by, den_out, vel_out, prs_out,
    columns, swept, rows_out, tiles_out, out_sem,
):
    n_rows, n_x = den_out.shape[1:]
    n_tiles = n_x // LANES
    groups = n_rows // SUB + 2
    n_steps = LANES // SUB
    top = [got[k * SUB : (k + 1) * SUB, :] for k in range(got.shape[0] // SUB)]
    while len(top) > 1:
        top = [jnp.maximum(x, y) for x, y in zip(top[::2], top[1::2])]
    dt = courant / jnp.max(top[0], axis=0, keepdims=True)

    def x_group(state, row, offsets, block, late):
        o = pl.ds(row, SUB)

        def tile_of(n, t):
            return state[n, o, (t + REACH) * LANES : (t + REACH + 1) * LANES]

        width, inv_w, amount, step, face, gaps, flux, result = {}, {}, {}, {}, {}, {}, {}, {}
        bits = offsets + float(SHIFT)
        high_bit = bits > 3.5
        low_bits = jnp.where(high_bit, 0.0, bits)
        mid_bit = low_bits > 1.5
        odd = low_bits - jnp.where(mid_bit, 2.0, 0.0) > 0.5
        once = {}

        def moved_one(j, f):
            if (j, f) not in once:
                once[j, f] = jnp.where(odd, result[j - 1][f], result[j][f])
            return once[j, f]

        def put(j):
            for f in range(5):
                v = jnp.where(mid_bit, moved_one(j, f), moved_one(j + 2, f))
                v = jnp.where(high_bit, result[j - 2][f], v)
                columns[block, f, pl.ds(j, SUB, stride=n_steps), :] = v

        def finish(i):
            kept = [tile_of(0, i)] + [amount[i][f] * width[i] for f in range(1, 5)]
            result[i] = primitive(*(kept[f] + flux[i - 1][f] - flux[i][f] for f in range(5)))
            if i < SHIFT:
                result[n_steps + i] = [wrapped(v, -1) for v in result[i]]
            if i >= n_steps - SHIFT:
                result[i - n_steps] = [wrapped(v, 1) for v in result[i]]

        def first():
            flux[-1] = [wrapped(v, 1) for v in flux[n_steps - 1]]
            finish(0)

        for t in range(-REACH, n_steps + 3):
            if t < n_steps + REACH:
                width[t] = 1.0 + dt * tile_of(2, t)
                inv_w[t] = inverse(width[t])
                lag = tile_of(0, t) * inv_w[t]
                amount[t] = (
                    lag, lag * (tile_of(3, t) - dt * tile_of(4, t)), lag * tile_of(5, t), lag * tile_of(6, t),
                    lag * (tile_of(7, t) - dt * tile_of(8, t)),
                )
            if late:
                late.pop(0)()
            i = t - 2
            c = t - 3
            if c >= 0:
                us = tile_of(1, c)
                up = us > 0.0
                d = dt * us
                weights = flux_weights(d, jnp.abs(d) * jnp.where(up, inv_w[c], inv_w[c + 1]))
                flux[c] = []
            step[i], face[i], gaps[i] = [], [], []
            for f in range(5):
                if -1 <= i < n_steps:
                    steps = step_and_gap(*(amount[i + k][f] for k in (-1, 0, 1, 2)))
                    step[i].append(steps[0])
                    face[i].append(steps[1])
                if 0 <= i < n_steps:
                    gaps[i].append(gaps_of(face[i][f], step[i][f], face[i - 1][f], step[i - 1][f]))
                if i == n_steps:
                    gaps[i].append([wrapped(v, -1) for v in gaps[0][f]])
                if c >= 0:
                    flux[c].append(flux_of(up, d, *weights, amount[c][f], gaps[c][f], amount[c + 1][f], gaps[c + 1][f]))
            if c >= 1:
                finish(c)
                if c >= 2 * SHIFT + 1:
                    put(c - SHIFT)
        late.append(first)
        for j in (n_steps - 2, n_steps - 1, 0, 1, 2):
            late.append(lambda j=j: put(j))

    def turn(n, f, first, second):
        natural = jnp.transpose(columns[n, f])
        for k in range(n_tiles):
            for h, group in enumerate((first, second)):
                at = (k * 2 + h) * SUB
                swept[f, pl.ds((group * n_tiles + k) * SUB, SUB), :] = natural[at : at + SUB, :]

    n_own = n_rows // PAIR
    late, turns = [], []
    x_group(halo_state, 0, halo_by[...], 0, late)
    for g in range(n_own):
        x_group(state, g * SUB, rows_by[g * SUB : (g + 1) * SUB, :], g + 1, late)
        if g == 0:
            turns = [(0, f, 0, groups - 1) for f in range(5)]
        else:
            turns = [(g, f, 2 * g - 1, 2 * g) for f in range(5)]
        for args in turns:
            turn(*args)
    for put_late in late:
        put_late()
    turns = [(n_own, f, 2 * n_own - 1, 2 * n_own) for f in range(5)]

    total = groups * SUB

    def load_row(r):
        at = (r // SUB) * n_tiles * SUB + r % SUB
        rho, ta, un, tb, p = (swept[f, pl.ds(at, SUB, stride=SUB), :] for f in range(5))
        return rho, un, ta, tb, p

    bits = lines_by[...] + float(SHIFT)
    high_bit = bits > 3.5
    low_bits = jnp.where(high_bit, 0.0, bits)
    mid_bit = low_bits > 1.5
    odd = low_bits - jnp.where(mid_bit, 2.0, 0.0) > 0.5
    once = {}

    def moved_one(i, f):
        if (i, f) not in once:
            once[i, f] = jnp.where(odd, done[i - 1][f], done[i][f])
        return once[i, f]

    cells, inv_rho, imp, faces, edges = {}, {}, {}, {}, {}
    stars, lags, weights, q_steps, q_faces, q_edges, fluxes, done = {}, {}, {}, {}, {}, {}, {}, {}
    copies, waiting = [], []
    targets = (den_out.at[0], vel_out.at[1, 0], vel_out.at[0, 0], vel_out.at[2, 0], prs_out.at[0])

    def turn_back(a, f):
        here = pl.ds(a * SUB, SUB)
        tiles = [rows_out[f, pl.ds((a * n_tiles + j) * SUB, SUB), :] for j in range(n_tiles)]
        for k, tile in enumerate(tiles):
            tiles_out[f, here, pl.ds(k * LANES, LANES)] = tile

    def send(a, f):
        here = pl.ds(a * SUB, SUB)
        copies.append(pltpu.make_async_copy(tiles_out.at[f, here, :], targets[f].at[here, :], out_sem.at[f, a]))
        copies[-1].start()

    def solve_row(r):
        if turns:
            turn(*turns.pop(0))
        cells[r] = load_row(r)
        rho, un, ta, tb, p = cells[r]
        inv_rho[r] = inverse(rho)
        imp[r] = sound_impedance(rho, inv_rho[r], p)
        i = r - 2
        if i >= 1:
            faces[i] = [face_of(*(cells[i + k][f] for k in (-1, 0, 1, 2))) for f in (1, 4)]
        if i >= 2:
            edges[i] = [edges_of(cells[i][f], faces[i - 1][n], faces[i][n]) for n, f in enumerate((1, 4))]
        i = r - 3
        if i >= 2:
            (_, u_right), (_, p_right) = edges[i]
            (u_left, _), (p_left, _) = edges[i + 1]
            us, ps = riemann(imp[i], imp[i + 1], u_right, u_left, p_right, p_left)
            stars[i] = us, ps, us * ps, dt * us
        if i >= 3:
            rho, un, ta, tb, p = cells[i]
            us, ps, work, d = stars[i]
            _, ps_b, work_b, d_b = stars[i - 1]
            w = 1.0 + d - d_b
            inv_w = inverse(w)
            rate = dt * inv_rho[i]
            lag = rho * inv_w
            e = total_energy(inv_rho[i], p, un, ta, tb)
            lags[i] = (
                lag, lag * (un - rate * (ps - ps_b)), lag * ta, lag * tb, lag * (e - rate * (work - work_b)),
            )
            weights[i] = w, inv_w

    def remap_row(r):
        i = r - 5
        n = r - 6
        if n >= 5:
            d = stars[n][3]
            up = d > 0.0
            near_far = flux_weights(d, jnp.abs(d) * jnp.where(up, weights[n][1], weights[n + 1][1]))
            fluxes[n] = []
        q_steps[i], q_faces[i], q_edges[i] = [], [], []
        for f in range(5):
            if i >= 4:
                step, face = step_and_gap(*(lags[i + k][f] for k in (-1, 0, 1, 2)))
                q_steps[i].append(step)
                q_faces[i].append(face)
            if i >= 5:
                q_edges[i].append(gaps_of(q_faces[i][f], q_steps[i][f], q_faces[i - 1][f], q_steps[i - 1][f]))
            if n >= 5:
                fluxes[n].append(
                    flux_of(up, d, *near_far, lags[n][f], q_edges[n][f], lags[n + 1][f], q_edges[n + 1][f])
                )
        i = n
        if i >= 6:
            done[i] = primitive(
                *(
                    (lags[i][f] * weights[i][0] if f else cells[i][0]) + fluxes[i - 1][f] - fluxes[i][f]
                    for f in range(5)
                )
            )
        i = r - 8
        if i >= HALO:
            j = i - HALO
            a, b = divmod(j, SUB)
            for f in range(5):
                v = jnp.where(mid_bit, moved_one(i, f), moved_one(i + 2, f))
                v = jnp.where(high_bit, done[i - 2][f], v)
                rows_out[f, pl.ds(a * n_tiles * SUB + b, SUB, stride=SUB), :] = v
            if b == SUB - 1:
                if a:
                    for f in range(5):
                        send(a - 1, f)
                waiting.extend((a, f) for f in range(5))
        if waiting:
            turn_back(*waiting.pop(0))

    for r in range(total + LEAD):
        if r < total:
            solve_row(r)
        if r >= LEAD:
            remap_row(r - LEAD)
    for f in range(5):
        if (n_rows // SUB - 1, f) in waiting:
            turn_back(n_rows // SUB - 1, f)
        send(n_rows // SUB - 1, f)
    for copy in copies:
        copy.wait()


def body(n_dev, n_cols, density, velocity, pressure, offsets_x, offsets_y):
    n_rows, n_x = density.shape[1:]
    f32 = jnp.float32
    vmem = pl.BlockSpec(memory_space=pltpu.VMEM)
    everyone = n_dev * n_cols
    small = pltpu.CompilerParams(vmem_limit_bytes=16 * 2**20)
    hbm = pl.BlockSpec(memory_space=pltpu.HBM)
    wide = 5 * n_x + LANES
    halo = jax.ShapeDtypeStruct((HALO, wide), f32)
    pay, up, down = pl.pallas_call(
        speed_kernel,
        out_shape=(jax.ShapeDtypeStruct((everyone, LANES), f32), halo, halo),
        in_specs=[hbm] * 4,
        out_specs=[hbm] * 3,
        scratch_shapes=[
            pltpu.VMEM((everyone, LANES), f32),
            pltpu.VMEM((n_rows, wide), f32),
            pltpu.VMEM(offsets_x.shape, jnp.int32),
            pltpu.VMEM((1, LANES), f32),
            pltpu.SemaphoreType.DMA((7,)),
            pltpu.SemaphoreType.DMA((3,)),
        ],
        compiler_params=pltpu.CompilerParams(vmem_limit_bytes=A_LIMIT),
    )(density, velocity, pressure, offsets_x)
    got = lax.all_to_all(pay, ("rows", "cols"), split_axis=0, concat_axis=0, tiled=True)
    before = lax.ppermute(up, "rows", [(i, (i + 1) % n_dev) for i in range(n_dev)])
    after = lax.ppermute(down, "rows", [(i, (i - 1) % n_dev) for i in range(n_dev)])
    long = (LANES // SUB + 2 * REACH) * LANES
    rooms = pltpu.VMEM((5, LANES, LANES), f32)
    n_own = n_rows // PAIR
    state, rows_by, lines_by = pl.pallas_call(
        own_kernel,
        out_shape=(
            jax.ShapeDtypeStruct((9, n_own * SUB, long), f32),
            jax.ShapeDtypeStruct((n_own * SUB, LANES), f32),
            jax.ShapeDtypeStruct((SUB, LANES), f32),
        ),
        in_specs=[vmem] * 5,
        out_specs=[vmem] * 3,
        scratch_shapes=[pltpu.VMEM((1, LANES), f32), pltpu.VMEM((n_own, 5, LANES, LANES), f32)],
        compiler_params=small,
        cost_estimate=pl.CostEstimate(flops=OWN_COST, bytes_accessed=10**6, transcendentals=0),
    )(density, velocity, pressure, offsets_x, offsets_y)
    halo_state, halo_by = pl.pallas_call(
        halo_kernel,
        out_shape=(
            jax.ShapeDtypeStruct((9, SUB, long), f32), jax.ShapeDtypeStruct((SUB, LANES), f32),
        ),
        in_specs=[vmem] * 2,
        out_specs=[vmem] * 2,
        scratch_shapes=[rooms],
        compiler_params=small,
        cost_estimate=pl.CostEstimate(flops=HALO_COST, bytes_accessed=10**6, transcendentals=0),
    )(before, after)
    plane = jax.ShapeDtypeStruct(density.shape, f32)
    tall = (n_rows + 2 * HALO) * n_x // LANES
    short = n_rows * n_x // LANES
    return pl.pallas_call(
        sweep_kernel,
        out_shape=(plane, jax.ShapeDtypeStruct(velocity.shape, f32), plane),
        in_specs=[vmem] * 6,
        out_specs=[hbm] * 3,
        scratch_shapes=[
            pltpu.VMEM((n_own + 1, 5, LANES, LANES), f32),
            pltpu.VMEM((5, tall, LANES), f32),
            pltpu.VMEM((5, short, LANES), f32),
            pltpu.VMEM((5, n_rows, n_x), f32),
            pltpu.SemaphoreType.DMA((5, n_rows // SUB)),
        ],
        compiler_params=small,
    )(state, halo_state, got, rows_by, halo_by, lines_by)


def solution(mesh):
    n_dev, n_cols = mesh.shape["rows"], mesh.shape["cols"]
    return jax.shard_map(
        lambda *arrays: body(n_dev, n_cols, *arrays),
        mesh=mesh,
        in_specs=(
            P("cols", "rows", None),
            P(None, "cols", "rows", None),
            P("cols", "rows", None),
            P("cols", "rows"),
            P("cols", None),
        ),
        out_specs=(P("cols", "rows", None), P(None, "cols", "rows", None), P("cols", "rows", None)),
        check_vma=False,
    )
```
